32 devices in a mesh: blk: 8 (over y, x, core), sig: 4 (over z).
Axes of the slice: x: 2, y: 2, z: 4, core: 2. Of those that a mesh axis runs over, the one named last changes fastest.
Arguments:
- coarse_fields: float32 [4096, 3, 512], P(('blk', 'sig')), may hold values from -6 to 6
- fine_fields: float32 [1024, 3, 8, 512], P(('blk', 'sig')), may hold values from -6 to 6
- owner: int32 [1024, 1], P(('blk', 'sig')), may hold values from 0 to 7, as said below
- target_tile: int32 [1024, 1], P(('blk', 'sig')), may hold values from 0 to 127, as said below
- tags: int32 [4096, 512], P(('blk', 'sig')), may hold values 0 or 1
Outputs:
- synced: float32 [4096, 3, 512], P(('blk', 'sig'))
- signature: float32 [8, 1032], P('blk')
The draws below stay inside these ranges and needn't reach their ends.
Inputs may be any that keep to these rules, and one draw needn't show every extreme that they name: On the 32 patches of one device at most 16 name the same owner; in every sig slab some devices name one owner exactly 16 times. `target_tile`: among the patches of all devices with one sig index no owner and tile is named twice; in every sig slab one owner has all 128 of its tiles named.
All inputs are finite; a program needn't handle non-finite values. No bound on the sum of `tags` on one device may be relied on, other than what follows from the above.
Results may differ from the reference program's by a relative error of at most 0.0002.
Values sent between devices are 32-bit elements; how exact they have to be, the bound alone decides.
A program may use at most 64 MiB of HBM per device.

```python
import jax
import jax.numpy as jnp

EDGE = 8
CELLS = 512
TILES_DEV = 128
PATCH_DEV = 32
CAP = 16
TILES = 4096
PATCHES = 1024
N_BLK = 8
N_SIG = 4


def plan_patches(key):
    base = jax.random.fold_in(key, 4111)
    streams = jax.random.split(base, 5)
    heavy = jax.random.randint(streams[0], (N_SIG, 1, 1), 0, N_BLK).astype(jnp.int32)
    source_ids = jnp.arange(N_BLK, dtype=jnp.int32)[None, :]
    rank_scores = jax.random.randint(streams[1], (N_SIG, N_BLK), 0, 65536).astype(jnp.int32) * N_BLK + source_ids
    sources_sorted = jnp.argsort(rank_scores, axis=1)
    source_rank = jnp.argsort(sources_sorted, axis=1).astype(jnp.int32)
    heavy_share = jnp.clip(TILES_DEV - CAP * source_rank, 0, CAP)[:, :, None]
    offset = jax.random.randint(streams[2], (N_SIG, N_BLK, 1), 0, N_BLK - 1).astype(jnp.int32)
    position = jnp.arange(PATCH_DEV, dtype=jnp.int32)[None, None, :]
    spread = (offset + position - heavy_share) % (N_BLK - 1)
    logical = jnp.where(position < heavy_share, heavy, (heavy + 1 + spread) % N_BLK)
    position_scores = jax.random.randint(streams[3], (N_SIG, N_BLK, PATCH_DEV), 0, 65536).astype(jnp.int32) * PATCH_DEV + position
    shuffle = jnp.argsort(position_scores, axis=2)
    owners = jnp.take_along_axis(logical, shuffle, axis=2).astype(jnp.int32)
    flat_owner = owners.reshape(N_SIG, N_BLK * PATCH_DEV)
    matches = (flat_owner[:, :, None] == jnp.arange(N_BLK, dtype=jnp.int32)[None, None, :]).astype(jnp.int32)
    earlier = jnp.cumsum(matches, axis=1) - matches
    arrival = jnp.sum(earlier * matches, axis=2).astype(jnp.int32)
    tile_ids = jnp.arange(TILES_DEV, dtype=jnp.int32)[None, None, :]
    tile_scores = jax.random.randint(streams[4], (N_SIG, N_BLK, TILES_DEV), 0, 65536).astype(jnp.int32) * TILES_DEV + tile_ids
    tile_order = jnp.argsort(tile_scores, axis=2).astype(jnp.int32).reshape(N_SIG, N_BLK * TILES_DEV)
    target = jnp.take_along_axis(tile_order, flat_owner * TILES_DEV + arrival, axis=1).astype(jnp.int32)
    owner_out = jnp.transpose(owners, (1, 0, 2)).reshape(PATCHES, 1)
    target_out = jnp.transpose(target.reshape(N_SIG, N_BLK, PATCH_DEV), (1, 0, 2)).reshape(PATCHES, 1)
    return (owner_out.astype(jnp.int32), target_out.astype(jnp.int32))


def draw_owner(key, part):
    return plan_patches(key)[0]


def draw_target_tile(key, part):
    return plan_patches(key)[1]


def touch_ends(result, own_key, low, largest):
    place = [jax.random.randint(jax.random.fold_in(own_key, axis), (), 0, length) for axis, length in enumerate(result.shape)]
    longest = result.shape.index(max(result.shape))
    next_to = place[:longest] + [(place[longest] + 1) % result.shape[longest]] + place[longest + 1:]
    return result.at[tuple(place)].set(low).at[tuple(next_to)].set(largest)


def levels(own_key, dims, cuts, low, largest):
    def one(dim, blocks):
        steps = jax.random.uniform(jax.random.fold_in(jax.random.fold_in(own_key, 6), dim), (blocks,), jnp.float32, low / len(cuts), largest / len(cuts))
        return jnp.repeat(jnp.exp(steps), dims[dim] // blocks).reshape((-1,) + (1,) * (len(dims) - dim - 1))

    level = one(*cuts[0])
    for cut in cuts[1:]:
        level = level * one(*cut)
    return level


def scatter_about(stream_key, extent, deviation, bound, pieces=(), kind=jnp.bfloat16):
    entries = deviation * jax.random.normal(stream_key, extent, jnp.float32)
    if pieces:
        entries = entries * levels(stream_key, extent, pieces, -0.22, 0.18)
    return jnp.clip(entries, -bound, bound).astype(kind)


def setup_inputs(seed: int = 0) -> dict:
    key_list = jax.random.split(jax.random.key(seed), 6)
    return {
        "coarse_fields": scatter_about(key_list[0], (TILES, 3, CELLS), 1.0, 6.0, ((0, 32),), jnp.float32),
        "fine_fields": scatter_about(key_list[1], (PATCHES, 3, 8, CELLS), 1.0, 6.0, ((0, 32),), jnp.float32),
        "owner": draw_owner(jax.random.fold_in(key_list[5], 71), 0),
        "target_tile": draw_target_tile(jax.random.fold_in(key_list[5], 71), 0),
        "tags": touch_ends((jax.random.randint(key_list[4], (TILES, CELLS), 0, 2) < 1).astype(jnp.int32), jax.random.fold_in(key_list[4], 1), 0, 1),
    }


def indicator_of(fields):
    total = jnp.zeros(fields.shape[:1] + fields.shape[2:], jnp.float32)
    for axis_number in (2, 3, 4):
        upper = jax.lax.slice_in_dim(fields, 2, EDGE, axis=axis_number)
        lower = jax.lax.slice_in_dim(fields, 0, EDGE - 2, axis=axis_number)
        middle = 0.5 * (upper - lower)
        widths = [(0, 0)] * 5
        widths[axis_number] = (1, 1)
        padded = jnp.pad(middle, widths)
        total = total + jnp.sum(padded * padded, axis=1)
    return total


def reference(coarse_fields, fine_fields, owner, target_tile, tags):
    averaged = (0.125 * jnp.sum(fine_fields, axis=2)).reshape(PATCHES, 3 * CELLS)
    device = jnp.arange(PATCHES, dtype=jnp.int32) // PATCH_DEV
    slab = device % N_SIG
    tile_ids = ((owner[:, 0] * N_SIG + slab) * TILES_DEV + target_tile[:, 0]).astype(jnp.int32)
    totals = jax.ops.segment_sum(averaged, tile_ids, num_segments=TILES)
    covered = jax.ops.segment_sum(jnp.ones((PATCHES,), jnp.float32), tile_ids, num_segments=TILES)
    flat = coarse_fields.reshape(TILES, 3 * CELLS)
    synced = jnp.where(covered[:, None] > 0, totals, flat)
    synced = synced.reshape(TILES, 3, CELLS)
    indicator = indicator_of(synced.reshape(TILES, 3, EDGE, EDGE, EDGE))
    weight = tags.reshape(TILES, EDGE, EDGE, EDGE).astype(jnp.float32) * indicator
    weight = weight.reshape(N_BLK, N_SIG, TILES_DEV, EDGE, EDGE, EDGE)
    along_y = jnp.sum(weight, axis=(1, 3, 5)).reshape(N_BLK, TILES_DEV * EDGE) / (EDGE * EDGE * N_SIG)
    along_z = jnp.sum(weight, axis=(1, 2, 3, 4)) / (EDGE * EDGE * TILES_DEV * N_SIG)
    signature = jnp.concatenate([along_y, along_z], axis=1)
    return synced, signature
```

```python
import functools

import jax
import jax.numpy as jnp
from jax import lax
from jax.experimental import pallas as pl
from jax.experimental.pallas import tpu as pltpu
from jax.sharding import PartitionSpec as P

EDGE = 8
FIELDS = 3
MESH = pl.DeviceIdType.MESH


def plan(blocks):
    if blocks == 8:
        steps = {
            "x0": (0, 0, 1, 2, 2, None),
            "y1": (0, 1, 1, 4, 4, None),
            "x1": (0, 1, 1, 2, 2, None),
            "y0": (0, 0, 1, 4, 4, None),
            "c": (0, 0, 2, 1, 1, None),
            "d0": (2, 0, 1, 4, 6, "x0"),
            "d1": (4, 1, 1, 2, 6, "y1"),
            "cx0": (2, 0, 1, 1, 3, "x0"),
            "cy1": (4, 1, 1, 1, 5, "y1"),
            "cx1": (2, 1, 1, 1, 3, "x1"),
            "cy0": (4, 0, 1, 1, 5, "y0"),
            "cd0": (6, 0, 1, 1, 7, "d0"),
            "cd1": (6, 1, 1, 1, 7, "d1"),
        }
        return steps
    return None


def kernel(
    blocks, slabs,
    coarse_hbm, fine_hbm, owner_hbm, target_hbm, tags_hbm,
    synced_ref, sig_ref,
    fine, coarse, tags, own_i, tgt_i, meta, rec, turned, tags_t, parts,
    load_sem, msend, mrecv, dsend, drecv, ssend, srecv,
):
    tile_count = coarse.shape[1]
    cells = coarse.shape[2]
    patches = fine.shape[0]
    half = patches // 2
    me = lax.axis_index("blk")
    slab = lax.axis_index("sig")

    def partner(mask):
        index = me
        bit = 1
        while bit <= mask:
            if mask & bit:
                index = index + bit - 2 * bit * ((me // bit) % 2)
            bit *= 2
        return index

    def load(k, src, dst):
        copy = pltpu.make_async_copy(src, dst, load_sem.at[k])
        copy.start()
        return copy

    load_owner = load(0, owner_hbm, own_i)
    load_target = load(1, target_hbm, tgt_i)
    load_fine = [
        load(2 + h, fine_hbm.at[pl.ds(h * half, half)], fine.at[pl.ds(h * half, half)]) for h in range(2)
    ]
    load_tags = load(4, tags_hbm, tags)
    load_coarse = load(5, coarse_hbm, coarse)

    barrier = pltpu.get_barrier_semaphore()
    for mask in range(1, blocks):
        pl.semaphore_signal(barrier, inc=1, device_id={"blk": partner(mask)}, device_id_type=MESH)
    for shift in range(1, slabs):
        pl.semaphore_signal(
            barrier, inc=1, device_id={"sig": lax.rem(slab + shift, slabs)}, device_id_type=MESH
        )

    load_owner.wait()
    load_target.wait()
    code = own_i[...] * tile_count + tgt_i[...]
    wide = jnp.concatenate([code] * (128 // patches), axis=1).astype(jnp.float32)
    meta[0] = jnp.broadcast_to(wide, (8, 128))

    def average(h):
        load_fine[h].wait()
        for f in range(FIELDS):
            rec[0, h, f] = 0.125 * jnp.sum(fine[h * half : (h + 1) * half, f], axis=1)

    average(0)
    pl.semaphore_wait(barrier, blocks - 1 + slabs - 1)

    started = []

    def send(src, dst, send_sem, recv_sem, device):
        copy = pltpu.make_async_remote_copy(
            src_ref=src, dst_ref=dst, send_sem=send_sem, recv_sem=recv_sem,
            device_id=device, device_id_type=MESH,
        )
        copy.start()
        started.append(copy)
        return copy

    def split(x):
        high = x.astype(jnp.bfloat16)
        low = (x - high.astype(jnp.float32)).astype(jnp.bfloat16)
        return jnp.concatenate([high, low], axis=0)

    lane = lax.broadcasted_iota(jnp.int32, (tile_count, 4 * patches), 1)
    first = (lane // patches) % 2 == 0
    tile_codes = (
        lax.broadcasted_iota(jnp.int32, (tile_count, 4 * patches), 0) + me * tile_count
    ).astype(jnp.float32)

    def place(group):
        codes = jnp.where(first, meta[2 * group][0:1], meta[2 * group + 1][0:1])
        return jnp.where(codes == tile_codes, 1.0, 0.0).astype(jnp.float32)

    def add(group):
        chosen = place(group).astype(jnp.bfloat16)
        for f in range(FIELDS):
            rows = rec[pl.ds(2 * group, 2), :, f].reshape(2 * patches, cells)
            synced_ref[f] += jnp.dot(chosen, split(rows), preferred_element_type=jnp.float32)

    def prepare():
        load_tags.wait()
        tags_t[...] = (0.25 * tags[...].astype(jnp.float32)).T.reshape(tags_t.shape)
        for copy in metas:
            copy.wait_recv()
        if blocks <= 8:
            hits = place(0)
            for group in range(1, blocks // 2):
                hits = hits + place(group)
        else:
            hits = lax.fori_loop(
                0, blocks // 2, lambda group, total: total + place(group),
                jnp.zeros((tile_count, 4 * patches), jnp.float32),
            )
        free = jnp.max(hits, axis=1, keepdims=True) == 0
        load_coarse.wait()
        for f in range(FIELDS):
            synced_ref[f] = jnp.where(free, coarse[f], 0.0)

    steps = plan(blocks)
    metas = []

    def send_metas():
        for mask in range(1, blocks):
            metas.append(
                send(meta.at[0], meta.at[mask], msend.at[mask], mrecv.at[mask], {"blk": partner(mask)})
            )

    if steps is not None:
        names = list(steps)
        copies = {}

        def go(name):
            slot, start, count, mask, target, _ = steps[name]
            k = names.index(name)
            copies[name] = send(
                rec.at[slot, pl.ds(start, count)], rec.at[target, pl.ds(start, count)],
                dsend.at[k], drecv.at[k], {"blk": partner(mask)},
            )

        go("x0")
        go("y0")
        send_metas()
        average(1)
        go("y1")
        go("x1")
        go("c")
        prepare()
        copies["x0"].wait_recv()
        go("d0")
        go("cx0")
        copies["y1"].wait_recv()
        go("d1")
        go("cy1")
        copies["c"].wait_recv()
        add(0)
        copies["y0"].wait_recv()
        go("cy0")
        copies["x1"].wait_recv()
        go("cx1")
        copies["cx0"].wait_recv()
        copies["cx1"].wait_recv()
        add(1)
        copies["cy0"].wait_recv()
        copies["cy1"].wait_recv()
        add(2)
        copies["d0"].wait_recv()
        go("cd0")
        copies["d1"].wait_recv()
        go("cd1")
        copies["cd0"].wait_recv()
        copies["cd1"].wait_recv()
        add(3)
    else:
        send_metas()
        average(1)
        bit, k = 1, 0
        while bit < blocks:
            send(
                rec.at[pl.ds(0, bit)], rec.at[pl.ds(bit, bit)], dsend.at[k], drecv.at[k], {"blk": partner(bit)}
            ).wait_recv()
            bit, k = 2 * bit, k + 1
        prepare()

        def body(group, carry):
            add(group)
            return carry

        lax.fori_loop(0, blocks // 2, body, 0)

    for f in range(FIELDS):
        turned[f] = synced_ref[f].T.reshape(turned.shape[1:])

    depth = lax.broadcasted_iota(jnp.int32, (EDGE, EDGE, tile_count), 1)
    inner_z = (depth > 0) & (depth < EDGE - 1)
    total = jnp.zeros((EDGE, EDGE, tile_count), jnp.float32)
    edge_row = jnp.zeros((1, EDGE, tile_count), jnp.float32)
    for x in range(EDGE):
        sum_x = sum_y = sum_z = None
        for f in range(FIELDS):
            mid = turned[f, x]
            dy = mid[2:] - mid[:-2]
            dz = mid - pltpu.roll(mid, 2, 1)
            sum_y = dy * dy if f == 0 else sum_y + dy * dy
            sum_z = dz * dz if f == 0 else sum_z + dz * dz
            if 0 < x < EDGE - 1:
                dx = turned[f, x + 1] - turned[f, x - 1]
                sum_x = dx * dx if f == 0 else sum_x + dx * dx
        value = jnp.where(inner_z, pltpu.roll(sum_z, EDGE - 1, 1), 0.0)
        value = value + jnp.concatenate([edge_row, sum_y, edge_row], axis=0)
        if sum_x is not None:
            value = value + sum_x
        total = total + tags_t[x] * value

    parts[slab, 0] = jnp.sum(total, axis=1)
    parts[slab, 1] = jnp.sum(total, axis=0)
    sums = []
    for shift in range(1, slabs):
        sums.append(
            send(
                parts.at[slab], parts.at[slab], ssend.at[shift], srecv.at[shift],
                {"sig": lax.rem(slab + shift, slabs)},
            )
        )
    for shift in range(1, slabs):
        came = lax.rem(slab + slabs - shift, slabs)
        pltpu.make_async_remote_copy(
            src_ref=parts.at[came], dst_ref=parts.at[came], send_sem=ssend.at[shift], recv_sem=srecv.at[shift],
            device_id={"sig": lax.rem(slab + shift, slabs)}, device_id_type=MESH,
        ).wait_recv()
    whole = parts[0]
    for k in range(1, slabs):
        whole = whole + parts[k]

    along_y = whole[0] * (1.0 / (EDGE * EDGE * slabs))
    along_z = whole[1] * (1.0 / (EDGE * EDGE * tile_count * slabs))
    group = 128 // EDGE
    spread = jnp.concatenate([along_y] * group, axis=0)
    row = lax.broadcasted_iota(jnp.int32, (128, tile_count), 0)
    col = lax.broadcasted_iota(jnp.int32, (128, tile_count), 1)
    spread = jnp.where(col % group == row // EDGE, spread, 0.0)
    lines = tile_count // group
    pick = (
        lax.broadcasted_iota(jnp.int32, (lines, tile_count), 1) // group
        == lax.broadcasted_iota(jnp.int32, (lines, tile_count), 0)
    ).astype(jnp.float32)
    across = (((1,), (1,)), ((), ()))
    order = lax.dot_general(
        pick, spread, across, precision=lax.Precision.HIGHEST, preferred_element_type=jnp.float32
    )
    last = lax.dot_general(
        jnp.ones((8, tile_count), jnp.float32), along_z, across,
        precision=lax.Precision.HIGHEST, preferred_element_type=jnp.float32,
    )
    for r in range(lines):
        sig_ref[0:1, r * 128 : (r + 1) * 128] = order[r : r + 1]
    sig_ref[0:1, lines * 128 : lines * 128 + EDGE] = last[0:1]

    for copy in started:
        copy.wait_send()


def shards(blocks, slabs, coarse_fields, fine_fields, owner, target_tile, tags):
    tile_count, _, cells = coarse_fields.shape
    patches = fine_fields.shape[0]
    coarse = jnp.transpose(coarse_fields, (1, 0, 2))
    anywhere = pl.BlockSpec(memory_space=pl.ANY)
    vmem = pl.BlockSpec(memory_space=pltpu.VMEM)
    copies = 16
    f32 = jnp.float32
    synced, signature = pl.pallas_call(
        functools.partial(kernel, blocks, slabs),
        out_shape=(
            jax.ShapeDtypeStruct((FIELDS, tile_count, cells), f32),
            jax.ShapeDtypeStruct((1, tile_count * EDGE + EDGE), f32),
        ),
        in_specs=[anywhere] * 5,
        out_specs=(vmem, vmem),
        scratch_shapes=[
            pltpu.VMEM(fine_fields.shape, f32),
            pltpu.VMEM((FIELDS, tile_count, cells), f32),
            pltpu.VMEM((tile_count, cells), jnp.int32),
            pltpu.VMEM((1, patches), jnp.int32),
            pltpu.VMEM((1, patches), jnp.int32),
            pltpu.VMEM((blocks, 8, 128), f32),
            pltpu.VMEM((blocks, 2, FIELDS, patches // 2, cells), f32),
            pltpu.VMEM((FIELDS, EDGE, EDGE, EDGE, tile_count), f32),
            pltpu.VMEM((EDGE, EDGE, EDGE, tile_count), f32),
            pltpu.VMEM((slabs, 2, EDGE, tile_count), f32),
            pltpu.SemaphoreType.DMA((6,)),
            pltpu.SemaphoreType.DMA((blocks,)),
            pltpu.SemaphoreType.DMA((blocks,)),
            pltpu.SemaphoreType.DMA((copies,)),
            pltpu.SemaphoreType.DMA((copies,)),
            pltpu.SemaphoreType.DMA((slabs,)),
            pltpu.SemaphoreType.DMA((slabs,)),
        ],
        compiler_params=pltpu.CompilerParams(
            collective_id=0, has_side_effects=True, vmem_limit_bytes=32 * 1024 * 1024
        ),
        name="average_down",
    )(coarse, fine_fields, owner.reshape(1, patches), target_tile.reshape(1, patches), tags)
    return jnp.transpose(synced, (1, 0, 2)), signature


def solution(mesh):
    blocks, slabs = mesh.shape["blk"], mesh.shape["sig"]
    return jax.shard_map(
        functools.partial(shards, blocks, slabs),
        mesh=mesh,
        in_specs=(
            P(("blk", "sig"), None, None),
            P(("blk", "sig"), None, None, None),
            P(("blk", "sig"), None),
            P(("blk", "sig"), None),
            P(("blk", "sig"), None),
        ),
        out_specs=(P(("blk", "sig"), None, None), P("blk", None)),
        check_vma=False,
    )
```

```python
import functools

import jax
import jax.numpy as jnp
from jax import lax
from jax.experimental import pallas as pl
from jax.experimental.pallas import tpu as pltpu
from jax.sharding import PartitionSpec as P

EDGE = 8
FIELDS = 3
VMEM_BYTES = 62 * 1024 * 1024
MESH = pl.DeviceIdType.MESH


def kernel(
    blocks, slabs,
    coarse_hbm, fine_hbm, owner_hbm, target_hbm, tags_hbm,
    synced_hbm, sums_ref,
    synced_ref, fine, coarse, tags, own_i, tgt_i, meta, rec, turned, tags_t, total, parts,
    load_sem, out_sem, msend, mrecv, dsend, drecv, ssend, srecv,
):
    tile_count = coarse.shape[1]
    cells = coarse.shape[2]
    patches = fine.shape[1]
    me = lax.axis_index("blk")
    slab = lax.axis_index("sig")

    def partner(mask):
        index = me
        bit = 1
        while bit <= mask:
            if mask & bit:
                index = index + bit - 2 * bit * ((me // bit) % 2)
            bit *= 2
        return index

    def load(k, src, dst):
        copy = pltpu.make_async_copy(src, dst, load_sem.at[k])
        copy.start()
        return copy

    load_fine = [load(f, fine_hbm.at[:, f], fine.at[f]) for f in range(FIELDS)]
    load_owner = load(FIELDS, owner_hbm, own_i)
    load_target = load(FIELDS + 1, target_hbm, tgt_i)
    load_tags = load(FIELDS + 2, tags_hbm, tags)
    load_coarse = load(FIELDS + 3, coarse_hbm, coarse)

    barrier = pltpu.get_barrier_semaphore()
    for mask in range(1, blocks):
        pl.semaphore_signal(barrier, inc=1, device_id={"blk": partner(mask)}, device_id_type=MESH)
    for shift in range(1, slabs):
        pl.semaphore_signal(
            barrier, inc=1, device_id={"sig": lax.rem(slab + shift, slabs)}, device_id_type=MESH
        )

    def split(x):
        high = x.astype(jnp.bfloat16)
        return high, (x - high.astype(jnp.float32)).astype(jnp.bfloat16)

    mean = jnp.where(
        lax.broadcasted_iota(jnp.int32, (patches, patches * 8), 1) // 8
        == lax.broadcasted_iota(jnp.int32, (patches, patches * 8), 0),
        0.125, 0.0,
    ).astype(jnp.bfloat16)

    def average(f):
        load_fine[f].wait()
        high, low = split(fine[f].reshape(patches * 8, cells))
        rows = jnp.dot(mean, high, preferred_element_type=jnp.float32)
        rows = rows + jnp.dot(mean, low, preferred_element_type=jnp.float32)
        rec[0, f] = rows.reshape(rec.shape[2:])

    average(0)
    load_owner.wait()
    load_target.wait()
    code = own_i[...] * tile_count + tgt_i[...]
    wide = jnp.concatenate([code] * (128 // patches), axis=1).astype(jnp.float32)
    meta[0] = jnp.broadcast_to(wide, (8, 128))
    pl.semaphore_wait(barrier, blocks - 1 + slabs - 1)

    started = []
    writes = []

    def send(src, dst, send_sem, recv_sem, device):
        copy = pltpu.make_async_remote_copy(
            src_ref=src, dst_ref=dst, send_sem=send_sem, recv_sem=recv_sem,
            device_id=device, device_id_type=MESH,
        )
        copy.start()
        started.append(copy)
        return copy

    lane = lax.broadcasted_iota(jnp.int32, (tile_count, 4 * patches), 1)
    first = (lane // patches) % 2 == 0
    tile_codes = (
        lax.broadcasted_iota(jnp.int32, (tile_count, 4 * patches), 0) + me * tile_count
    ).astype(jnp.float32)

    def place(group):
        codes = jnp.where(first, meta[2 * group][0:1], meta[2 * group + 1][0:1])
        return jnp.where(codes == tile_codes, 1.0, 0.0).astype(jnp.float32)

    def add(group, f):
        rows = rec[pl.ds(2 * group, 2), f].reshape(2 * patches, cells)
        synced_ref[f] += jnp.dot(
            place(group).astype(jnp.bfloat16), jnp.concatenate(split(rows), axis=0),
            preferred_element_type=jnp.float32,
        )

    def prepare():
        load_tags.wait()
        tags_t[...] = (0.25 * tags[...].astype(jnp.float32)).T.reshape(tags_t.shape)
        total[...] = jnp.zeros_like(total)
        for copy in metas:
            copy.wait_recv()
        if blocks <= 8:
            hits = place(0)
            for group in range(1, blocks // 2):
                hits = hits + place(group)
        else:
            hits = lax.fori_loop(
                0, blocks // 2, lambda group, found: found + place(group),
                jnp.zeros((tile_count, 4 * patches), jnp.float32),
            )
        free = jnp.max(hits, axis=1, keepdims=True) == 0
        load_coarse.wait()
        for f in range(FIELDS):
            synced_ref[f] = jnp.where(free, coarse[f], 0.0)

    depth = lax.broadcasted_iota(jnp.int32, (EDGE, EDGE, tile_count), 1)
    inner_z = (depth > 0) & (depth < EDGE - 1)
    edge_row = jnp.zeros((1, EDGE, tile_count), jnp.float32)

    def weigh(f):
        writes.append(pltpu.make_async_copy(synced_ref.at[f], synced_hbm.at[f], out_sem.at[f]))
        writes[-1].start()
        turned[...] = synced_ref[f].T.reshape(turned.shape)
        for x in range(EDGE):
            mid = turned[x]
            dy = mid[2:] - mid[:-2]
            dz = mid - pltpu.roll(mid, 2, 1)
            value = jnp.where(inner_z, pltpu.roll(dz * dz, EDGE - 1, 1), 0.0)
            value = value + jnp.concatenate([edge_row, dy * dy, edge_row], axis=0)
            if 0 < x < EDGE - 1:
                dx = turned[x + 1] - turned[x - 1]
                value = value + dx * dx
            total[...] += tags_t[x] * value

    metas = []

    def send_metas():
        for mask in range(1, blocks):
            metas.append(
                send(meta.at[0], meta.at[mask], msend.at[mask], mrecv.at[mask], {"blk": partner(mask)})
            )

    if blocks == 8:
        copies = {}

        def go(name, slot, start, count, mask, target, f):
            k = len(copies)
            copies[name, f] = send(
                rec.at[slot, f, pl.ds(start, count)], rec.at[target, f, pl.ds(start, count)],
                dsend.at[k], drecv.at[k], {"blk": partner(mask)},
            )

        def came(f, *names):
            for name in names:
                copies[name, f].wait_recv()

        def own(f):
            go("x0", 0, 0, 1, 2, 2, f)
            go("y1", 0, 1, 1, 4, 4, f)
            go("x1", 0, 1, 1, 2, 2, f)
            go("y0", 0, 0, 1, 4, 4, f)
            go("c", 0, 0, 2, 1, 1, f)

        def forward(f):
            came(f, "x0")
            go("d0", 2, 0, 1, 4, 6, f)
            go("cx0", 2, 0, 1, 1, 3, f)
            came(f, "y1")
            go("d1", 4, 1, 1, 2, 6, f)
            go("cy1", 4, 1, 1, 1, 5, f)

        def share(f):
            came(f, "x1")
            go("cx1", 2, 1, 1, 1, 3, f)
            came(f, "y0")
            go("cy0", 4, 0, 1, 1, 5, f)

        def share_diagonal(f):
            came(f, "d0")
            go("cd0", 6, 0, 1, 1, 7, f)
            came(f, "d1")
            go("cd1", 6, 1, 1, 1, 7, f)

        def add_near(f):
            came(f, "c")
            add(0, f)
            came(f, "cx0", "cx1")
            add(1, f)
            came(f, "cy0", "cy1")
            add(2, f)

        def add_diagonal(f):
            came(f, "cd0", "cd1")
            add(3, f)

        own(0)
        send_metas()
        average(1)
        own(1)
        average(2)
        prepare()
        forward(0)
        own(2)
        share(0)
        forward(1)
        add_near(0)
        share(1)
        share_diagonal(0)
        forward(2)
        add_near(1)
        share(2)
        add_diagonal(0)
        weigh(0)
        share_diagonal(1)
        add_near(2)
        share_diagonal(2)
        add_diagonal(1)
        weigh(1)
        add_diagonal(2)
        weigh(2)
    else:
        send_metas()
        average(1)
        average(2)
        bit, k = 1, 0
        while bit < blocks:
            send(
                rec.at[pl.ds(0, bit)], rec.at[pl.ds(bit, bit)], dsend.at[k], drecv.at[k], {"blk": partner(bit)}
            ).wait_recv()
            bit, k = 2 * bit, k + 1
        prepare()

        def body(group, carry):
            for f in range(FIELDS):
                add(group, f)
            return carry

        lax.fori_loop(0, blocks // 2, body, 0)
        for f in range(FIELDS):
            weigh(f)

    parts[slab, 0] = jnp.sum(total[...], axis=1)
    parts[slab, 1] = jnp.sum(total[...], axis=0)
    for shift in range(1, slabs):
        send(
            parts.at[slab], parts.at[slab], ssend.at[shift], srecv.at[shift],
            {"sig": lax.rem(slab + shift, slabs)},
        )
    for shift in range(1, slabs):
        source = lax.rem(slab + slabs - shift, slabs)
        pltpu.make_async_remote_copy(
            src_ref=parts.at[source], dst_ref=parts.at[source], send_sem=ssend.at[shift], recv_sem=srecv.at[shift],
            device_id={"sig": lax.rem(slab + shift, slabs)}, device_id_type=MESH,
        ).wait_recv()
    whole = parts[0]
    for k in range(1, slabs):
        whole = whole + parts[k]
    sums_ref[...] = whole

    for copy in started:
        copy.wait_send()
    for copy in writes:
        copy.wait()


def finish(slabs, synced_in, sums, synced_out, signature, line, sem):
    write = pltpu.make_async_copy(synced_in, synced_out, sem.at[0])
    write.start()
    tile_count = sums.shape[2]
    along_y = sums[0] * (1.0 / (EDGE * EDGE * slabs))
    along_z = sums[1] * (1.0 / (EDGE * EDGE * tile_count * slabs))
    group = 128 // EDGE
    spread = jnp.concatenate([along_y] * group, axis=0)
    row = lax.broadcasted_iota(jnp.int32, (128, tile_count), 0)
    col = lax.broadcasted_iota(jnp.int32, (128, tile_count), 1)
    spread = jnp.where(col % group == row // EDGE, spread, 0.0)
    lines = tile_count // group
    pick = (
        lax.broadcasted_iota(jnp.int32, (lines, tile_count), 1) // group
        == lax.broadcasted_iota(jnp.int32, (lines, tile_count), 0)
    ).astype(jnp.float32)
    across = (((1,), (1,)), ((), ()))
    order = lax.dot_general(
        pick, spread, across, precision=lax.Precision.HIGHEST, preferred_element_type=jnp.float32
    )
    last = lax.dot_general(
        jnp.ones((8, tile_count), jnp.float32), along_z, across,
        precision=lax.Precision.HIGHEST, preferred_element_type=jnp.float32,
    )
    for r in range(lines):
        line[0:1, r * 128 : (r + 1) * 128] = order[r : r + 1]
    line[0:1, lines * 128 : lines * 128 + EDGE] = last[0:1]
    write_line = pltpu.make_async_copy(line, signature, sem.at[1])
    write_line.start()
    write_line.wait()
    write.wait()


def shards(blocks, slabs, coarse_fields, fine_fields, owner, target_tile, tags):
    tile_count, _, cells = coarse_fields.shape
    patches = fine_fields.shape[0]
    coarse = jnp.transpose(coarse_fields, (1, 0, 2))
    stay = pl.BlockSpec(memory_space=pl.ANY)
    vmem = pl.BlockSpec(memory_space=pltpu.VMEM)
    copies = 13 * FIELDS
    f32 = jnp.float32
    synced, sums = pl.pallas_call(
        functools.partial(kernel, blocks, slabs),
        out_shape=(
            jax.ShapeDtypeStruct((FIELDS, tile_count, cells), f32),
            jax.ShapeDtypeStruct((2, EDGE, tile_count), f32),
        ),
        in_specs=[stay] * 5,
        out_specs=(stay, vmem),
        scratch_shapes=[
            pltpu.VMEM((FIELDS, tile_count, cells), f32),
            pltpu.VMEM((FIELDS, patches, 8, cells), f32),
            pltpu.VMEM((FIELDS, tile_count, cells), f32),
            pltpu.VMEM((tile_count, cells), jnp.int32),
            pltpu.VMEM((1, patches), jnp.int32),
            pltpu.VMEM((1, patches), jnp.int32),
            pltpu.VMEM((blocks, 8, 128), f32),
            pltpu.VMEM((blocks, FIELDS, 2, patches // 2, cells), f32),
            pltpu.VMEM((EDGE, EDGE, EDGE, tile_count), f32),
            pltpu.VMEM((EDGE, EDGE, EDGE, tile_count), f32),
            pltpu.VMEM((EDGE, EDGE, tile_count), f32),
            pltpu.VMEM((slabs, 2, EDGE, tile_count), f32),
            pltpu.SemaphoreType.DMA((FIELDS + 4,)),
            pltpu.SemaphoreType.DMA((FIELDS,)),
            pltpu.SemaphoreType.DMA((blocks,)),
            pltpu.SemaphoreType.DMA((blocks,)),
            pltpu.SemaphoreType.DMA((copies,)),
            pltpu.SemaphoreType.DMA((copies,)),
            pltpu.SemaphoreType.DMA((slabs,)),
            pltpu.SemaphoreType.DMA((slabs,)),
        ],
        compiler_params=pltpu.CompilerParams(
            collective_id=0, has_side_effects=True, vmem_limit_bytes=VMEM_BYTES
        ),
        name="average_down",
    )(coarse, fine_fields, owner.reshape(1, patches), target_tile.reshape(1, patches), tags)
    width = tile_count * EDGE + EDGE
    synced, signature = pl.pallas_call(
        functools.partial(finish, slabs),
        out_shape=(
            jax.ShapeDtypeStruct((FIELDS, tile_count, cells), f32),
            jax.ShapeDtypeStruct((1, width), f32),
        ),
        in_specs=[stay, vmem],
        out_specs=(stay, stay),
        scratch_shapes=[pltpu.VMEM((1, width), f32), pltpu.SemaphoreType.DMA((2,))],
        compiler_params=pltpu.CompilerParams(vmem_limit_bytes=VMEM_BYTES),
        name="write_outputs",
    )(synced, sums)
    return jnp.transpose(synced, (1, 0, 2)), signature


def solution(mesh):
    blocks, slabs = mesh.shape["blk"], mesh.shape["sig"]
    return jax.shard_map(
        functools.partial(shards, blocks, slabs),
        mesh=mesh,
        in_specs=(
            P(("blk", "sig"), None, None),
            P(("blk", "sig"), None, None, None),
            P(("blk", "sig"), None),
            P(("blk", "sig"), None),
            P(("blk", "sig"), None),
        ),
        out_specs=(P(("blk", "sig"), None, None), P("blk", None)),
        check_vma=False,
    )
```

```python
import functools

import jax
import jax.numpy as jnp
from jax import lax
from jax.experimental import pallas as pl
from jax.experimental.pallas import tpu as pltpu
from jax.sharding import PartitionSpec as P

EDGE = 8
FIELDS = 3
VMEM_BYTES = 32 * 1024 * 1024
MESH = pl.DeviceIdType.MESH


def kernel(
    blocks, slabs,
    coarse_hbm, fine_hbm, owner_hbm, target_hbm, tags_hbm,
    synced_ref, sums_ref,
    fine, coarse, tags, own_i, tgt_i, meta, rec, turned, tags_t, total, parts,
    load_sem, msend, mrecv, dsend, drecv, ssend, srecv,
):
    tile_count = coarse.shape[1]
    cells = coarse.shape[2]
    patches = fine.shape[1]
    me = lax.axis_index("blk")
    slab = lax.axis_index("sig")

    def partner(mask):
        index = me
        bit = 1
        while bit <= mask:
            if mask & bit:
                index = index + bit - 2 * bit * ((me // bit) % 2)
            bit *= 2
        return index

    def load(k, src, dst):
        copy = pltpu.make_async_copy(src, dst, load_sem.at[k])
        copy.start()
        return copy

    load_fine = [load(f, fine_hbm.at[:, f], fine.at[f]) for f in range(FIELDS)]
    load_owner = load(FIELDS, owner_hbm, own_i)
    load_target = load(FIELDS + 1, target_hbm, tgt_i)
    load_tags = load(FIELDS + 2, tags_hbm, tags)
    load_coarse = load(FIELDS + 3, coarse_hbm, coarse)

    barrier = pltpu.get_barrier_semaphore()
    for mask in range(1, blocks):
        pl.semaphore_signal(barrier, inc=1, device_id={"blk": partner(mask)}, device_id_type=MESH)
    for shift in range(1, slabs):
        pl.semaphore_signal(
            barrier, inc=1, device_id={"sig": lax.rem(slab + shift, slabs)}, device_id_type=MESH
        )

    def split(x):
        high = x.astype(jnp.bfloat16)
        return high, (x - high.astype(jnp.float32)).astype(jnp.bfloat16)

    mean = jnp.where(
        lax.broadcasted_iota(jnp.int32, (patches, patches * 8), 1) // 8
        == lax.broadcasted_iota(jnp.int32, (patches, patches * 8), 0),
        0.125, 0.0,
    ).astype(jnp.bfloat16)

    def average(f):
        load_fine[f].wait()
        high, low = split(fine[f].reshape(patches * 8, cells))
        rows = jnp.dot(mean, high, preferred_element_type=jnp.float32)
        rows = rows + jnp.dot(mean, low, preferred_element_type=jnp.float32)
        rec[0, f] = rows.reshape(rec.shape[2:])

    average(0)
    load_owner.wait()
    load_target.wait()
    code = own_i[...] * tile_count + tgt_i[...]
    wide = jnp.concatenate([code] * (128 // patches), axis=1).astype(jnp.float32)
    meta[0] = jnp.broadcast_to(wide, (8, 128))
    pl.semaphore_wait(barrier, blocks - 1 + slabs - 1)

    started = []

    def send(src, dst, send_sem, recv_sem, device):
        copy = pltpu.make_async_remote_copy(
            src_ref=src, dst_ref=dst, send_sem=send_sem, recv_sem=recv_sem,
            device_id=device, device_id_type=MESH,
        )
        copy.start()
        started.append(copy)
        return copy

    lane = lax.broadcasted_iota(jnp.int32, (tile_count, 4 * patches), 1)
    first = (lane // patches) % 2 == 0
    tile_codes = (
        lax.broadcasted_iota(jnp.int32, (tile_count, 4 * patches), 0) + me * tile_count
    ).astype(jnp.float32)

    def place(group):
        codes = jnp.where(first, meta[2 * group][0:1], meta[2 * group + 1][0:1])
        return jnp.where(codes == tile_codes, 1.0, 0.0).astype(jnp.float32)

    def add(group, f):
        rows = rec[pl.ds(2 * group, 2), f].reshape(2 * patches, cells)
        synced_ref[f] += jnp.dot(
            place(group).astype(jnp.bfloat16), jnp.concatenate(split(rows), axis=0),
            preferred_element_type=jnp.float32,
        )

    def turn_tags():
        load_tags.wait()
        tags_t[...] = (0.25 * tags[...].astype(jnp.float32)).T.reshape(tags_t.shape)
        total[...] = jnp.zeros_like(total)

    def prepare():
        for copy in metas:
            copy.wait_recv()
        if blocks <= 8:
            hits = place(0)
            for group in range(1, blocks // 2):
                hits = hits + place(group)
        else:
            hits = lax.fori_loop(
                0, blocks // 2, lambda group, found: found + place(group),
                jnp.zeros((tile_count, 4 * patches), jnp.float32),
            )
        free = jnp.max(hits, axis=1, keepdims=True) == 0
        load_coarse.wait()
        for f in range(FIELDS):
            synced_ref[f] = jnp.where(free, coarse[f], 0.0)

    depth = lax.broadcasted_iota(jnp.int32, (EDGE, EDGE, tile_count), 1)
    inner_z = (depth > 0) & (depth < EDGE - 1)
    edge_row = jnp.zeros((1, EDGE, tile_count), jnp.float32)

    def weigh(f):
        turned[...] = synced_ref[f].T.reshape(turned.shape)
        for x in range(EDGE):
            mid = turned[x]
            dy = mid[2:] - mid[:-2]
            dz = mid - pltpu.roll(mid, 2, 1)
            value = jnp.where(inner_z, pltpu.roll(dz * dz, EDGE - 1, 1), 0.0)
            value = value + jnp.concatenate([edge_row, dy * dy, edge_row], axis=0)
            if 0 < x < EDGE - 1:
                dx = turned[x + 1] - turned[x - 1]
                value = value + dx * dx
            total[...] += tags_t[x] * value

    metas = []

    def send_metas():
        for mask in range(1, blocks):
            metas.append(
                send(meta.at[0], meta.at[mask], msend.at[mask], mrecv.at[mask], {"blk": partner(mask)})
            )

    if blocks == 8:
        copies = {}

        def go(name, slot, start, count, mask, target, f):
            k = len(copies)
            copies[name, f] = send(
                rec.at[slot, f, pl.ds(start, count)], rec.at[target, f, pl.ds(start, count)],
                dsend.at[k], drecv.at[k], {"blk": partner(mask)},
            )

        def came(f, *names):
            for name in names:
                copies[name, f].wait_recv()

        def own(f):
            go("x0", 0, 0, 1, 2, 2, f)
            go("y1", 0, 1, 1, 4, 4, f)
            go("x1", 0, 1, 1, 2, 2, f)
            go("y0", 0, 0, 1, 4, 4, f)
            go("c", 0, 0, 2, 1, 1, f)

        def forward(f):
            came(f, "x0")
            go("d0", 2, 0, 1, 4, 6, f)
            came(f, "y1")
            go("d1", 4, 1, 1, 2, 6, f)

        def share(f):
            came(f, "x1")
            go("cx", 2, 0, 2, 1, 3, f)
            came(f, "y0")
            go("cy", 4, 0, 2, 1, 5, f)

        def share_diagonal(f):
            came(f, "d0")
            go("cd0", 6, 0, 1, 1, 7, f)
            came(f, "d1")
            go("cd1", 6, 1, 1, 1, 7, f)

        def drain(*later):
            kept = [copies[name, FIELDS - 1] for name in later if (name, FIELDS - 1) in copies]
            for copy in started:
                if not any(copy is other for other in kept):
                    copy.wait_send()
            started[:] = kept

        def add_near(f):
            came(f, "c")
            add(0, f)
            came(f, "cx")
            add(1, f)
            came(f, "cy")
            add(2, f)

        def add_diagonal(f):
            came(f, "cd0", "cd1")
            add(3, f)

        own(0)
        send_metas()
        average(1)
        own(1)
        average(2)
        forward(0)
        own(2)
        turn_tags()
        share(0)
        prepare()
        forward(1)
        add_near(0)
        share(1)
        share_diagonal(0)
        forward(2)
        add_near(1)
        share(2)
        add_diagonal(0)
        weigh(0)
        share_diagonal(1)
        add_near(2)
        drain("d0", "d1", "cd0", "cd1")
        share_diagonal(2)
        add_diagonal(1)
        weigh(1)
        add_diagonal(2)
        weigh(2)
    else:
        send_metas()
        average(1)
        average(2)
        bit, k = 1, 0
        while bit < blocks:
            send(
                rec.at[pl.ds(0, bit)], rec.at[pl.ds(bit, bit)], dsend.at[k], drecv.at[k], {"blk": partner(bit)}
            ).wait_recv()
            bit, k = 2 * bit, k + 1
        turn_tags()
        prepare()

        def body(group, carry):
            for f in range(FIELDS):
                add(group, f)
            return carry

        lax.fori_loop(0, blocks // 2, body, 0)
        for f in range(FIELDS):
            weigh(f)

    parts[slab, 0] = jnp.sum(total[...], axis=1)
    parts[slab, 1] = jnp.sum(total[...], axis=0)
    for shift in range(1, slabs):
        send(
            parts.at[slab], parts.at[slab], ssend.at[shift], srecv.at[shift],
            {"sig": lax.rem(slab + shift, slabs)},
        )
    for shift in range(1, slabs):
        source = lax.rem(slab + slabs - shift, slabs)
        pltpu.make_async_remote_copy(
            src_ref=parts.at[source], dst_ref=parts.at[source], send_sem=ssend.at[shift], recv_sem=srecv.at[shift],
            device_id={"sig": lax.rem(slab + shift, slabs)}, device_id_type=MESH,
        ).wait_recv()
    whole = parts[0]
    for k in range(1, slabs):
        whole = whole + parts[k]
    sums_ref[...] = whole

    for copy in started:
        copy.wait_send()


def finish(slabs, synced_in, sums, synced_out, signature, line, sem):
    write = pltpu.make_async_copy(synced_in, synced_out, sem.at[0])
    write.start()
    tile_count = sums.shape[2]
    along_y = sums[0] * (1.0 / (EDGE * EDGE * slabs))
    along_z = sums[1] * (1.0 / (EDGE * EDGE * tile_count * slabs))
    group = 128 // EDGE
    spread = jnp.concatenate([along_y] * group, axis=0)
    row = lax.broadcasted_iota(jnp.int32, (128, tile_count), 0)
    col = lax.broadcasted_iota(jnp.int32, (128, tile_count), 1)
    spread = jnp.where(col % group == row // EDGE, spread, 0.0)
    lines = tile_count // group
    pick = (
        lax.broadcasted_iota(jnp.int32, (lines, tile_count), 1) // group
        == lax.broadcasted_iota(jnp.int32, (lines, tile_count), 0)
    ).astype(jnp.float32)
    across = (((1,), (1,)), ((), ()))
    order = lax.dot_general(
        pick, spread, across, precision=lax.Precision.HIGHEST, preferred_element_type=jnp.float32
    )
    last = lax.dot_general(
        jnp.ones((8, tile_count), jnp.float32), along_z, across,
        precision=lax.Precision.HIGHEST, preferred_element_type=jnp.float32,
    )
    for r in range(lines):
        line[0:1, r * 128 : (r + 1) * 128] = order[r : r + 1]
    line[0:1, lines * 128 : lines * 128 + EDGE] = last[0:1]
    write_line = pltpu.make_async_copy(line, signature, sem.at[1])
    write_line.start()
    write_line.wait()
    write.wait()


def shards(blocks, slabs, coarse_fields, fine_fields, owner, target_tile, tags):
    tile_count, _, cells = coarse_fields.shape
    patches = fine_fields.shape[0]
    coarse = jnp.transpose(coarse_fields, (1, 0, 2))
    stay = pl.BlockSpec(memory_space=pl.ANY)
    vmem = pl.BlockSpec(memory_space=pltpu.VMEM)
    copies = 11 * FIELDS
    f32 = jnp.float32
    synced, sums = pl.pallas_call(
        functools.partial(kernel, blocks, slabs),
        out_shape=(
            jax.ShapeDtypeStruct((FIELDS, tile_count, cells), f32),
            jax.ShapeDtypeStruct((2, EDGE, tile_count), f32),
        ),
        in_specs=[stay] * 5,
        out_specs=(vmem, vmem),
        scratch_shapes=[
            pltpu.VMEM((FIELDS, patches, 8, cells), f32),
            pltpu.VMEM((FIELDS, tile_count, cells), f32),
            pltpu.VMEM((tile_count, cells), jnp.int32),
            pltpu.VMEM((1, patches), jnp.int32),
            pltpu.VMEM((1, patches), jnp.int32),
            pltpu.VMEM((blocks, 8, 128), f32),
            pltpu.VMEM((blocks, FIELDS, 2, patches // 2, cells), f32),
            pltpu.VMEM((EDGE, EDGE, EDGE, tile_count), f32),
            pltpu.VMEM((EDGE, EDGE, EDGE, tile_count), f32),
            pltpu.VMEM((EDGE, EDGE, tile_count), f32),
            pltpu.VMEM((slabs, 2, EDGE, tile_count), f32),
            pltpu.SemaphoreType.DMA((FIELDS + 4,)),
            pltpu.SemaphoreType.DMA((blocks,)),
            pltpu.SemaphoreType.DMA((blocks,)),
            pltpu.SemaphoreType.DMA((copies,)),
            pltpu.SemaphoreType.DMA((copies,)),
            pltpu.SemaphoreType.DMA((slabs,)),
            pltpu.SemaphoreType.DMA((slabs,)),
        ],
        compiler_params=pltpu.CompilerParams(
            collective_id=0, has_side_effects=True, vmem_limit_bytes=VMEM_BYTES
        ),
        name="average_down",
    )(*[
        pltpu.with_memory_space_constraint(x, pltpu.HBM)
        for x in (coarse, fine_fields, owner.reshape(1, patches), target_tile.reshape(1, patches), tags)
    ])
    width = tile_count * EDGE + EDGE
    synced, signature = pl.pallas_call(
        functools.partial(finish, slabs),
        out_shape=(
            jax.ShapeDtypeStruct((FIELDS, tile_count, cells), f32),
            jax.ShapeDtypeStruct((1, width), f32),
        ),
        in_specs=[vmem, vmem],
        out_specs=(stay, stay),
        scratch_shapes=[pltpu.VMEM((1, width), f32), pltpu.SemaphoreType.DMA((2,))],
        name="write_outputs",
    )(synced, sums)
    return jnp.transpose(synced, (1, 0, 2)), signature


def solution(mesh):
    blocks, slabs = mesh.shape["blk"], mesh.shape["sig"]
    return jax.shard_map(
        functools.partial(shards, blocks, slabs),
        mesh=mesh,
        in_specs=(
            P(("blk", "sig"), None, None),
            P(("blk", "sig"), None, None, None),
            P(("blk", "sig"), None),
            P(("blk", "sig"), None),
            P(("blk", "sig"), None),
        ),
        out_specs=(P(("blk", "sig"), None, None), P("blk", None)),
        check_vma=False,
    )
```

```python
import functools

import jax
import jax.numpy as jnp
from jax import lax
from jax.experimental import pallas as pl
from jax.experimental.pallas import tpu as pltpu
from jax.sharding import PartitionSpec as P

EDGE = 8
FIELDS = 3
PIECES = 4
VMEM_BYTES = 32 * 1024 * 1024
MESH = pl.DeviceIdType.MESH


def kernel(
    blocks, slabs,
    coarse_hbm, fine_hbm, owner_hbm, target_hbm, tags_hbm,
    synced_ref, sums_ref,
    fine, coarse, tags, own_i, tgt_i, meta, rec, turned, tags_t, total, parts,
    load_sem, msend, mrecv, dsend, drecv, ssend, srecv,
):
    tile_count = coarse.shape[1]
    cells = coarse.shape[2]
    patches = fine.shape[1]
    me = lax.axis_index("blk")
    slab = lax.axis_index("sig")

    def partner(mask):
        index = me
        bit = 1
        while bit <= mask:
            if mask & bit:
                index = index + bit - 2 * bit * ((me // bit) % 2)
            bit *= 2
        return index

    def load(k, src, dst):
        copy = pltpu.make_async_copy(src, dst, load_sem.at[k])
        copy.start()
        return copy

    piece = patches // PIECES
    load_fine = [
        [
            load(f * PIECES + k, fine_hbm.at[pl.ds(k * piece, piece), f], fine.at[f, pl.ds(k * piece, piece)])
            for k in range(PIECES)
        ]
        for f in range(FIELDS)
    ]
    k = FIELDS * PIECES
    load_owner = load(k, owner_hbm, own_i)
    load_target = load(k + 1, target_hbm, tgt_i)
    load_tags = load(k + 2, tags_hbm, tags)
    load_coarse = [load(k + 3 + f, coarse_hbm.at[f], coarse.at[f]) for f in range(FIELDS)]

    barrier = pltpu.get_barrier_semaphore()
    for mask in range(1, blocks):
        pl.semaphore_signal(barrier, inc=1, device_id={"blk": partner(mask)}, device_id_type=MESH)
    for shift in range(1, slabs):
        pl.semaphore_signal(
            barrier, inc=1, device_id={"sig": lax.rem(slab + shift, slabs)}, device_id_type=MESH
        )

    def split(x):
        high = x.astype(jnp.bfloat16)
        return high, (x - high.astype(jnp.float32)).astype(jnp.bfloat16)

    mean = jnp.where(
        lax.broadcasted_iota(jnp.int32, (patches, patches * 8), 1) // 8
        == lax.broadcasted_iota(jnp.int32, (patches, patches * 8), 0),
        0.125, 0.0,
    ).astype(jnp.bfloat16)

    def average(f):
        for copy in load_fine[f]:
            copy.wait()
        high, low = split(fine[f].reshape(patches * 8, cells))
        rows = jnp.dot(mean, high, preferred_element_type=jnp.float32)
        rows = rows + jnp.dot(mean, low, preferred_element_type=jnp.float32)
        rec[0, f] = rows.reshape(rec.shape[2:])

    average(0)
    load_owner.wait()
    load_target.wait()
    code = own_i[...] * tile_count + tgt_i[...]
    wide = jnp.concatenate([code] * (128 // patches), axis=1).astype(jnp.float32)
    meta[0] = jnp.broadcast_to(wide, (8, 128))
    pl.semaphore_wait(barrier, blocks - 1 + slabs - 1)

    started = []

    def send(src, dst, send_sem, recv_sem, device):
        copy = pltpu.make_async_remote_copy(
            src_ref=src, dst_ref=dst, send_sem=send_sem, recv_sem=recv_sem,
            device_id=device, device_id_type=MESH,
        )
        copy.start()
        started.append(copy)
        return copy

    lane = lax.broadcasted_iota(jnp.int32, (tile_count, 4 * patches), 1)
    first = (lane // patches) % 2 == 0
    tile_codes = (
        lax.broadcasted_iota(jnp.int32, (tile_count, 4 * patches), 0) + me * tile_count
    ).astype(jnp.float32)

    def place(group):
        codes = jnp.where(first, meta[2 * group][0:1], meta[2 * group + 1][0:1])
        return jnp.where(codes == tile_codes, 1.0, 0.0).astype(jnp.float32)

    def add(group, f):
        rows = rec[pl.ds(2 * group, 2), f].reshape(2 * patches, cells)
        synced_ref[f] += jnp.dot(
            place(group).astype(jnp.bfloat16), jnp.concatenate(split(rows), axis=0),
            preferred_element_type=jnp.float32,
        )

    def turn_tags():
        load_tags.wait()
        tags_t[...] = (0.25 * tags[...].astype(jnp.float32)).T.reshape(tags_t.shape)
        total[...] = jnp.zeros_like(total)

    def prepare():
        for copy in metas:
            copy.wait_recv()
        if blocks <= 8:
            hits = place(0)
            for group in range(1, blocks // 2):
                hits = hits + place(group)
        else:
            hits = lax.fori_loop(
                0, blocks // 2, lambda group, found: found + place(group),
                jnp.zeros((tile_count, 4 * patches), jnp.float32),
            )
        free = jnp.max(hits, axis=1, keepdims=True) == 0
        for f in range(FIELDS):
            load_coarse[f].wait()
            synced_ref[f] = jnp.where(free, coarse[f], 0.0)

    depth = lax.broadcasted_iota(jnp.int32, (EDGE, EDGE, tile_count), 1)
    inner_z = (depth > 0) & (depth < EDGE - 1)
    edge_row = jnp.zeros((1, EDGE, tile_count), jnp.float32)

    def weigh(f):
        turned[...] = synced_ref[f].T.reshape(turned.shape)
        for x in range(EDGE):
            mid = turned[x]
            dy = mid[2:] - mid[:-2]
            dz = mid - pltpu.roll(mid, 2, 1)
            value = jnp.where(inner_z, pltpu.roll(dz * dz, EDGE - 1, 1), 0.0)
            value = value + jnp.concatenate([edge_row, dy * dy, edge_row], axis=0)
            if 0 < x < EDGE - 1:
                dx = turned[x + 1] - turned[x - 1]
                value = value + dx * dx
            total[...] += tags_t[x] * value

    metas = []

    def send_metas():
        for mask in range(1, blocks):
            metas.append(
                send(meta.at[0], meta.at[mask], msend.at[mask], mrecv.at[mask], {"blk": partner(mask)})
            )

    if blocks == 8:
        copies = {}

        def go(name, slot, start, count, mask, target, f):
            k = len(copies)
            copies[name, f] = send(
                rec.at[slot, f, pl.ds(start, count)], rec.at[target, f, pl.ds(start, count)],
                dsend.at[k], drecv.at[k], {"blk": partner(mask)},
            )

        def came(f, *names):
            for name in names:
                copies[name, f].wait_recv()

        def own(f):
            go("x0", 0, 0, 1, 2, 2, f)
            go("y1", 0, 1, 1, 4, 4, f)
            go("x1", 0, 1, 1, 2, 2, f)
            go("y0", 0, 0, 1, 4, 4, f)
            go("c", 0, 0, 2, 1, 1, f)

        def forward(f):
            came(f, "x0")
            go("d0", 2, 0, 1, 4, 6, f)
            came(f, "y1")
            go("d1", 4, 1, 1, 2, 6, f)

        def share(f):
            came(f, "x1")
            go("cx", 2, 0, 2, 1, 3, f)
            came(f, "y0")
            go("cy", 4, 0, 2, 1, 5, f)

        def share_diagonal(f):
            came(f, "d0")
            go("cd0", 6, 0, 1, 1, 7, f)
            came(f, "d1")
            go("cd1", 6, 1, 1, 1, 7, f)

        def drain(*later):
            kept = [copies[name, FIELDS - 1] for name in later if (name, FIELDS - 1) in copies]
            for copy in started:
                if not any(copy is other for other in kept):
                    copy.wait_send()
            started[:] = kept

        def add_near(f):
            came(f, "c")
            add(0, f)
            came(f, "cx")
            add(1, f)
            came(f, "cy")
            add(2, f)

        def add_diagonal(f):
            came(f, "cd0", "cd1")
            add(3, f)

        own(0)
        send_metas()
        average(1)
        own(1)
        average(2)
        forward(0)
        own(2)
        turn_tags()
        share(0)
        prepare()
        forward(1)
        add_near(0)
        share(1)
        share_diagonal(0)
        forward(2)
        add_near(1)
        share(2)
        add_diagonal(0)
        weigh(0)
        share_diagonal(1)
        add_near(2)
        drain("d0", "d1", "cd0", "cd1")
        share_diagonal(2)
        add_diagonal(1)
        weigh(1)
        add_diagonal(2)
        weigh(2)
    else:
        send_metas()
        average(1)
        average(2)
        bit, k = 1, 0
        while bit < blocks:
            send(
                rec.at[pl.ds(0, bit)], rec.at[pl.ds(bit, bit)], dsend.at[k], drecv.at[k], {"blk": partner(bit)}
            ).wait_recv()
            bit, k = 2 * bit, k + 1
        turn_tags()
        prepare()

        def body(group, carry):
            for f in range(FIELDS):
                add(group, f)
            return carry

        lax.fori_loop(0, blocks // 2, body, 0)
        for f in range(FIELDS):
            weigh(f)

    parts[slab, 0] = jnp.sum(total[...], axis=1)
    parts[slab, 1] = jnp.sum(total[...], axis=0)
    for shift in range(1, slabs):
        send(
            parts.at[slab], parts.at[slab], ssend.at[shift], srecv.at[shift],
            {"sig": lax.rem(slab + shift, slabs)},
        )
    for shift in range(1, slabs):
        source = lax.rem(slab + slabs - shift, slabs)
        pltpu.make_async_remote_copy(
            src_ref=parts.at[source], dst_ref=parts.at[source], send_sem=ssend.at[shift], recv_sem=srecv.at[shift],
            device_id={"sig": lax.rem(slab + shift, slabs)}, device_id_type=MESH,
        ).wait_recv()
    whole = parts[0]
    for k in range(1, slabs):
        whole = whole + parts[k]
    sums_ref[...] = whole

    for copy in started:
        copy.wait_send()


def finish(slabs, synced_in, sums, synced_out, signature, line, sem):
    tile_count = sums.shape[2]
    writes = []
    piece = tile_count // PIECES
    for f in range(FIELDS):
        for k in range(PIECES):
            rows = pl.ds(k * piece, piece)
            writes.append(
                pltpu.make_async_copy(
                    synced_in.at[f, rows], synced_out.at[f, rows], sem.at[1 + f * PIECES + k]
                )
            )
            writes[-1].start()
    along_y = sums[0] * (1.0 / (EDGE * EDGE * slabs))
    along_z = sums[1] * (1.0 / (EDGE * EDGE * tile_count * slabs))
    group = 128 // EDGE
    lines = tile_count // group
    spread = jnp.concatenate([along_y] * group, axis=0)
    row = lax.broadcasted_iota(jnp.int32, (128, tile_count), 0)
    col = lax.broadcasted_iota(jnp.int32, (128, tile_count), 1)
    spread = jnp.where(col % group == row // EDGE, spread, 0.0)
    terms = jnp.concatenate([spread, along_z], axis=0)
    high = terms.astype(jnp.bfloat16).astype(jnp.float32)
    terms = jnp.concatenate([high, terms - high], axis=1).astype(jnp.bfloat16)
    row = lax.broadcasted_iota(jnp.int32, (2 * lines, 2 * tile_count), 0)
    col = lax.broadcasted_iota(jnp.int32, (2 * lines, 2 * tile_count), 1) % tile_count
    pick = jnp.where((col // group == row) | (row >= lines), 1.0, 0.0).astype(jnp.bfloat16)
    order = lax.dot_general(pick, terms, (((1,), (1,)), ((), ())), preferred_element_type=jnp.float32)
    for r in range(lines):
        line[0:1, r * 128 : (r + 1) * 128] = order[r : r + 1, :128]
    line[0:1, lines * 128 : lines * 128 + EDGE] = order[lines : lines + 1, 128:]
    write_line = pltpu.make_async_copy(line, signature, sem.at[0])
    write_line.start()
    for copy in writes:
        copy.wait()
    write_line.wait()


def shards(blocks, slabs, coarse_fields, fine_fields, owner, target_tile, tags):
    tile_count, _, cells = coarse_fields.shape
    patches = fine_fields.shape[0]
    coarse = jnp.transpose(coarse_fields, (1, 0, 2))
    stay = pl.BlockSpec(memory_space=pl.ANY)
    vmem = pl.BlockSpec(memory_space=pltpu.VMEM)
    copies = 11 * FIELDS
    f32 = jnp.float32
    synced, sums = pl.pallas_call(
        functools.partial(kernel, blocks, slabs),
        out_shape=(
            jax.ShapeDtypeStruct((FIELDS, tile_count, cells), f32),
            jax.ShapeDtypeStruct((2, EDGE, tile_count), f32),
        ),
        in_specs=[stay] * 5,
        out_specs=(vmem, vmem),
        scratch_shapes=[
            pltpu.VMEM((FIELDS, patches, 8, cells), f32),
            pltpu.VMEM((FIELDS, tile_count, cells), f32),
            pltpu.VMEM((tile_count, cells), jnp.int32),
            pltpu.VMEM((1, patches), jnp.int32),
            pltpu.VMEM((1, patches), jnp.int32),
            pltpu.VMEM((blocks, 8, 128), f32),
            pltpu.VMEM((blocks, FIELDS, 2, patches // 2, cells), f32),
            pltpu.VMEM((EDGE, EDGE, EDGE, tile_count), f32),
            pltpu.VMEM((EDGE, EDGE, EDGE, tile_count), f32),
            pltpu.VMEM((EDGE, EDGE, tile_count), f32),
            pltpu.VMEM((slabs, 2, EDGE, tile_count), f32),
            pltpu.SemaphoreType.DMA((FIELDS * PIECES + 3 + FIELDS,)),
            pltpu.SemaphoreType.DMA((blocks,)),
            pltpu.SemaphoreType.DMA((blocks,)),
            pltpu.SemaphoreType.DMA((copies,)),
            pltpu.SemaphoreType.DMA((copies,)),
            pltpu.SemaphoreType.DMA((slabs,)),
            pltpu.SemaphoreType.DMA((slabs,)),
        ],
        compiler_params=pltpu.CompilerParams(
            collective_id=0, has_side_effects=True, vmem_limit_bytes=VMEM_BYTES
        ),
        name="average_down",
    )(*[
        pltpu.with_memory_space_constraint(x, pltpu.HBM)
        for x in (coarse, fine_fields, owner.reshape(1, patches), target_tile.reshape(1, patches), tags)
    ])
    width = tile_count * EDGE + EDGE
    synced, signature = pl.pallas_call(
        functools.partial(finish, slabs),
        out_shape=(
            jax.ShapeDtypeStruct((FIELDS, tile_count, cells), f32),
            jax.ShapeDtypeStruct((1, width), f32),
        ),
        in_specs=[vmem, vmem],
        out_specs=(stay, stay),
        scratch_shapes=[pltpu.VMEM((1, width), f32), pltpu.SemaphoreType.DMA((1 + FIELDS * PIECES,))],
        compiler_params=pltpu.CompilerParams(vmem_limit_bytes=4 * 1024 * 1024),
        name="write_outputs",
    )(synced, sums)
    return jnp.transpose(synced, (1, 0, 2)), signature


def solution(mesh):
    blocks, slabs = mesh.shape["blk"], mesh.shape["sig"]
    return jax.shard_map(
        functools.partial(shards, blocks, slabs),
        mesh=mesh,
        in_specs=(
            P(("blk", "sig"), None, None),
            P(("blk", "sig"), None, None, None),
            P(("blk", "sig"), None),
            P(("blk", "sig"), None),
            P(("blk", "sig"), None),
        ),
        out_specs=(P(("blk", "sig"), None, None), P("blk", None)),
        check_vma=False,
    )
```

```python
import functools

import jax
import jax.numpy as jnp
from jax import lax
from jax.experimental import pallas as pl
from jax.experimental.pallas import tpu as pltpu
from jax.sharding import PartitionSpec as P

EDGE = 8
FIELDS = 3
PIECES = 4
VMEM_BYTES = 32 * 1024 * 1024
MESH = pl.DeviceIdType.MESH


def kernel(
    blocks, slabs,
    coarse_hbm, fine_hbm, owner_hbm, target_hbm, tags_hbm,
    synced_ref, sums_ref,
    fine, coarse, tags, own_i, tgt_i, meta, rec, chosen, turned, tags_t, total, parts,
    load_sem, msend, mrecv, dsend, drecv, ssend, srecv,
):
    tile_count = coarse.shape[1]
    cells = coarse.shape[2]
    patches = fine.shape[1]
    me = lax.axis_index("blk")
    slab = lax.axis_index("sig")

    def partner(mask):
        index = me
        bit = 1
        while bit <= mask:
            if mask & bit:
                index = index + bit - 2 * bit * ((me // bit) % 2)
            bit *= 2
        return index

    def load(k, src, dst):
        copy = pltpu.make_async_copy(src, dst, load_sem.at[k])
        copy.start()
        return copy

    piece = patches // PIECES
    load_fine = [
        [
            load(f * PIECES + k, fine_hbm.at[pl.ds(k * piece, piece), f], fine.at[f, pl.ds(k * piece, piece)])
            for k in range(PIECES)
        ]
        for f in range(FIELDS)
    ]
    k = FIELDS * PIECES
    load_owner = load(k, owner_hbm, own_i)
    load_target = load(k + 1, target_hbm, tgt_i)
    load_tags = load(k + 2, tags_hbm, tags)
    load_coarse = [load(k + 3 + f, coarse_hbm.at[f], coarse.at[f]) for f in range(FIELDS)]

    barrier = pltpu.get_barrier_semaphore()
    for mask in range(1, blocks):
        pl.semaphore_signal(barrier, inc=1, device_id={"blk": partner(mask)}, device_id_type=MESH)
    for shift in range(1, slabs):
        pl.semaphore_signal(
            barrier, inc=1, device_id={"sig": lax.rem(slab + shift, slabs)}, device_id_type=MESH
        )

    def split(x):
        high = x.astype(jnp.bfloat16)
        return high, (x - high.astype(jnp.float32)).astype(jnp.bfloat16)

    mean = jnp.where(
        lax.broadcasted_iota(jnp.int32, (patches, patches * 8), 1) // 8
        == lax.broadcasted_iota(jnp.int32, (patches, patches * 8), 0),
        0.125, 0.0,
    ).astype(jnp.bfloat16)

    def average(f):
        for copy in load_fine[f]:
            copy.wait()
        high, low = split(fine[f].reshape(patches * 8, cells))
        rows = jnp.dot(mean, high, preferred_element_type=jnp.float32)
        rows = rows + jnp.dot(mean, low, preferred_element_type=jnp.float32)
        rec[0, f] = rows.reshape(rec.shape[2:])

    for f in range(FIELDS - 1):
        average(f)
    load_owner.wait()
    load_target.wait()
    code = own_i[...] * tile_count + tgt_i[...]
    wide = jnp.concatenate([code] * (128 // patches), axis=1).astype(jnp.float32)
    meta[0] = jnp.broadcast_to(wide, (8, 128))
    pl.semaphore_wait(barrier, blocks - 1 + slabs - 1)

    started = []

    def send(src, dst, send_sem, recv_sem, device):
        copy = pltpu.make_async_remote_copy(
            src_ref=src, dst_ref=dst, send_sem=send_sem, recv_sem=recv_sem,
            device_id=device, device_id_type=MESH,
        )
        copy.start()
        started.append(copy)
        return copy

    lane = lax.broadcasted_iota(jnp.int32, (1, 4 * patches), 1) // patches
    tile_codes = (
        lax.broadcasted_iota(jnp.int32, (tile_count, 4 * patches), 0) + me * tile_count
    ).astype(jnp.float32)

    def place(slots):
        codes = meta[slots[0]][0:1]
        for k in range(1, 4):
            codes = jnp.where(lane == k, meta[slots[k]][0:1], codes)
        return jnp.where(codes == tile_codes, 1.0, 0.0).astype(jnp.float32)

    def add(chosen, slot, count, f):
        rows = rec[pl.ds(slot, count), f].reshape(count * patches, cells)
        synced_ref[f] += jnp.dot(
            chosen, jnp.concatenate(split(rows), axis=0), preferred_element_type=jnp.float32
        )

    def turn_tags():
        load_tags.wait()
        tags_t[...] = (0.25 * tags[...].astype(jnp.float32)).T.reshape(tags_t.shape)
        total[...] = jnp.zeros_like(total)

    def prepare():
        for copy in metas:
            copy.wait_recv()
        if blocks == 8:
            hits = None
            for k, slots in enumerate(((0, 1, 2, 3), (4, 5, 0, 1), (2, 3, 4, 5), (6, 7, 6, 7))):
                found = place(slots)
                chosen[:, k * 128 : (k + 1) * 128] = found.astype(jnp.bfloat16)
                hits = found if hits is None else jnp.maximum(hits, found)
        else:
            hits = lax.fori_loop(
                0, blocks // 4, lambda k, found: found + place([4 * k, 4 * k + 1, 4 * k + 2, 4 * k + 3]),
                jnp.zeros((tile_count, 4 * patches), jnp.float32),
            )
        free = jnp.max(hits, axis=1, keepdims=True) == 0
        for f in range(FIELDS):
            load_coarse[f].wait()
            synced_ref[f] = jnp.where(free, coarse[f], 0.0)

    depth = lax.broadcasted_iota(jnp.int32, (EDGE, EDGE, tile_count), 1)
    inner_z = (depth > 0) & (depth < EDGE - 1)
    edge_row = jnp.zeros((1, EDGE, tile_count), jnp.float32)

    def weigh(f):
        turned[...] = synced_ref[f].T.reshape(turned.shape)
        for x in range(EDGE):
            mid = turned[x]
            dy = mid[2:] - mid[:-2]
            dz = mid - pltpu.roll(mid, 2, 1)
            value = jnp.where(inner_z, pltpu.roll(dz * dz, EDGE - 1, 1), 0.0)
            value = value + jnp.concatenate([edge_row, dy * dy, edge_row], axis=0)
            if 0 < x < EDGE - 1:
                dx = turned[x + 1] - turned[x - 1]
                value = value + dx * dx
            total[...] += tags_t[x] * value

    metas = []

    def send_metas():
        for mask in range(1, blocks):
            metas.append(
                send(meta.at[0], meta.at[mask], msend.at[mask], mrecv.at[mask], {"blk": partner(mask)})
            )

    if blocks == 8:
        copies = {}

        def go(name, slot, start, count, mask, target, part):
            k = len(copies)
            low, high = part
            fields, halves = pl.ds(low, high - low), pl.ds(start, count)
            copies[name, part] = send(
                rec.at[slot, fields, halves], rec.at[target, fields, halves],
                dsend.at[k], drecv.at[k], {"blk": partner(mask)},
            )

        def came(part, *names):
            for name in names:
                copies[name, part].wait_recv()

        def own(part):
            go("x0", 0, 0, 1, 2, 2, part)
            go("y1", 0, 1, 1, 4, 4, part)
            go("x1", 0, 1, 1, 2, 2, part)
            go("y0", 0, 0, 1, 4, 4, part)
            go("c", 0, 0, 2, 1, 1, part)

        def forward(part):
            came(part, "x0")
            go("d0", 2, 0, 1, 4, 6, part)
            came(part, "y1")
            go("d1", 4, 1, 1, 2, 6, part)

        def share(part):
            came(part, "x1")
            go("cx", 2, 0, 2, 1, 3, part)
            came(part, "y0")
            go("cy", 4, 0, 2, 1, 5, part)

        def share_diagonal(part):
            came(part, "d0")
            go("cd0", 6, 0, 1, 1, 7, part)
            came(part, "d1")
            go("cd1", 6, 1, 1, 1, 7, part)

        def drain(part, *later):
            kept = [copies[name, part] for name in later if (name, part) in copies]
            for copy in started:
                if not any(copy is other for other in kept):
                    copy.wait_send()
            started[:] = kept

        def add_near(part):
            came(part, "c", "cx", "cy")
            for f in range(*part):
                add(chosen[:, :384], 0, 6, f)

        def add_diagonal(part):
            came(part, "cd0", "cd1")
            for f in range(*part):
                add(chosen[:, 384:], 6, 2, f)

        early, late = (0, FIELDS - 1), (FIELDS - 1, FIELDS)
        own(early)
        send_metas()
        average(FIELDS - 1)
        own(late)
        turn_tags()
        forward(early)
        share(early)
        forward(late)
        prepare()
        share(late)
        add_near(early)
        share_diagonal(early)
        add_near(late)
        add_diagonal(early)
        drain(late, "d0", "d1")
        share_diagonal(late)
        for f in range(*early):
            weigh(f)
        add_diagonal(late)
        weigh(FIELDS - 1)
    else:
        send_metas()
        average(FIELDS - 1)
        bit, k = 1, 0
        while bit < blocks:
            send(
                rec.at[pl.ds(0, bit)], rec.at[pl.ds(bit, bit)], dsend.at[k], drecv.at[k], {"blk": partner(bit)}
            ).wait_recv()
            bit, k = 2 * bit, k + 1
        turn_tags()
        prepare()

        def body(group, carry):
            pair = place([2 * group, 2 * group + 1, 2 * group, 2 * group + 1]).astype(jnp.bfloat16)
            for f in range(FIELDS):
                add(pair, 2 * group, 2, f)
            return carry

        lax.fori_loop(0, blocks // 2, body, 0)
        for f in range(FIELDS):
            weigh(f)

    parts[slab, 0] = jnp.sum(total[...], axis=1)
    parts[slab, 1] = jnp.sum(total[...], axis=0)
    for shift in range(1, slabs):
        send(
            parts.at[slab], parts.at[slab], ssend.at[shift], srecv.at[shift],
            {"sig": lax.rem(slab + shift, slabs)},
        )
    for shift in range(1, slabs):
        source = lax.rem(slab + slabs - shift, slabs)
        pltpu.make_async_remote_copy(
            src_ref=parts.at[source], dst_ref=parts.at[source], send_sem=ssend.at[shift], recv_sem=srecv.at[shift],
            device_id={"sig": lax.rem(slab + shift, slabs)}, device_id_type=MESH,
        ).wait_recv()
    whole = parts[0]
    for k in range(1, slabs):
        whole = whole + parts[k]
    sums_ref[...] = whole

    for copy in started:
        copy.wait_send()


def finish(slabs, synced_in, sums, synced_out, signature, line, sem):
    tile_count = sums.shape[2]
    writes = []
    piece = tile_count // PIECES
    for f in range(FIELDS):
        for k in range(PIECES):
            rows = pl.ds(k * piece, piece)
            writes.append(
                pltpu.make_async_copy(
                    synced_in.at[f, rows], synced_out.at[f, rows], sem.at[1 + f * PIECES + k]
                )
            )
            writes[-1].start()
    along_y = sums[0] * (1.0 / (EDGE * EDGE * slabs))
    along_z = sums[1] * (1.0 / (EDGE * EDGE * tile_count * slabs))
    group = 128 // EDGE
    lines = tile_count // group
    spread = jnp.concatenate([along_y] * group, axis=0)
    row = lax.broadcasted_iota(jnp.int32, (128, tile_count), 0)
    col = lax.broadcasted_iota(jnp.int32, (128, tile_count), 1)
    spread = jnp.where(col % group == row // EDGE, spread, 0.0)
    terms = jnp.concatenate([spread, along_z], axis=0)
    high = terms.astype(jnp.bfloat16).astype(jnp.float32)
    terms = jnp.concatenate([high, terms - high], axis=1).astype(jnp.bfloat16)
    row = lax.broadcasted_iota(jnp.int32, (2 * lines, 2 * tile_count), 0)
    col = lax.broadcasted_iota(jnp.int32, (2 * lines, 2 * tile_count), 1) % tile_count
    pick = jnp.where((col // group == row) | (row >= lines), 1.0, 0.0).astype(jnp.bfloat16)
    order = lax.dot_general(pick, terms, (((1,), (1,)), ((), ())), preferred_element_type=jnp.float32)
    for r in range(lines):
        line[0:1, r * 128 : (r + 1) * 128] = order[r : r + 1, :128]
    line[0:1, lines * 128 : lines * 128 + EDGE] = order[lines : lines + 1, 128:]
    write_line = pltpu.make_async_copy(line, signature, sem.at[0])
    write_line.start()
    for copy in writes:
        copy.wait()
    write_line.wait()


def shards(blocks, slabs, coarse_fields, fine_fields, owner, target_tile, tags):
    tile_count, _, cells = coarse_fields.shape
    patches = fine_fields.shape[0]
    coarse = jnp.transpose(coarse_fields, (1, 0, 2))
    stay = pl.BlockSpec(memory_space=pl.ANY)
    vmem = pl.BlockSpec(memory_space=pltpu.VMEM)
    copies = 22
    f32 = jnp.float32
    synced, sums = pl.pallas_call(
        functools.partial(kernel, blocks, slabs),
        out_shape=(
            jax.ShapeDtypeStruct((FIELDS, tile_count, cells), f32),
            jax.ShapeDtypeStruct((2, EDGE, tile_count), f32),
        ),
        in_specs=[stay] * 5,
        out_specs=(vmem, vmem),
        scratch_shapes=[
            pltpu.VMEM((FIELDS, patches, 8, cells), f32),
            pltpu.VMEM((FIELDS, tile_count, cells), f32),
            pltpu.VMEM((tile_count, cells), jnp.int32),
            pltpu.VMEM((1, patches), jnp.int32),
            pltpu.VMEM((1, patches), jnp.int32),
            pltpu.VMEM((blocks, 8, 128), f32),
            pltpu.VMEM((blocks, FIELDS, 2, patches // 2, cells), f32),
            pltpu.VMEM((tile_count, 512), jnp.bfloat16),
            pltpu.VMEM((EDGE, EDGE, EDGE, tile_count), f32),
            pltpu.VMEM((EDGE, EDGE, EDGE, tile_count), f32),
            pltpu.VMEM((EDGE, EDGE, tile_count), f32),
            pltpu.VMEM((slabs, 2, EDGE, tile_count), f32),
            pltpu.SemaphoreType.DMA((FIELDS * PIECES + 3 + FIELDS,)),
            pltpu.SemaphoreType.DMA((blocks,)),
            pltpu.SemaphoreType.DMA((blocks,)),
            pltpu.SemaphoreType.DMA((copies,)),
            pltpu.SemaphoreType.DMA((copies,)),
            pltpu.SemaphoreType.DMA((slabs,)),
            pltpu.SemaphoreType.DMA((slabs,)),
        ],
        compiler_params=pltpu.CompilerParams(
            collective_id=0, has_side_effects=True, vmem_limit_bytes=VMEM_BYTES
        ),
        name="average_down",
    )(*[
        pltpu.with_memory_space_constraint(x, pltpu.HBM)
        for x in (coarse, fine_fields, owner.reshape(1, patches), target_tile.reshape(1, patches), tags)
    ])
    width = tile_count * EDGE + EDGE
    synced, signature = pl.pallas_call(
        functools.partial(finish, slabs),
        out_shape=(
            jax.ShapeDtypeStruct((FIELDS, tile_count, cells), f32),
            jax.ShapeDtypeStruct((1, width), f32),
        ),
        in_specs=[vmem, vmem],
        out_specs=(stay, stay),
        scratch_shapes=[pltpu.VMEM((1, width), f32), pltpu.SemaphoreType.DMA((1 + FIELDS * PIECES,))],
        compiler_params=pltpu.CompilerParams(vmem_limit_bytes=4 * 1024 * 1024),
        name="write_outputs",
    )(synced, sums)
    return jnp.transpose(synced, (1, 0, 2)), signature


def solution(mesh):
    blocks, slabs = mesh.shape["blk"], mesh.shape["sig"]
    return jax.shard_map(
        functools.partial(shards, blocks, slabs),
        mesh=mesh,
        in_specs=(
            P(("blk", "sig"), None, None),
            P(("blk", "sig"), None, None, None),
            P(("blk", "sig"), None),
            P(("blk", "sig"), None),
            P(("blk", "sig"), None),
        ),
        out_specs=(P(("blk", "sig"), None, None), P("blk", None)),
        check_vma=False,
    )
```

```python
import functools

import jax
import jax.numpy as jnp
from jax import lax
from jax.experimental import pallas as pl
from jax.experimental.pallas import tpu as pltpu
from jax.sharding import PartitionSpec as P

EDGE = 8
FIELDS = 3
PIECES = 4
VMEM_BYTES = 32 * 1024 * 1024
MESH = pl.DeviceIdType.MESH


def kernel(
    blocks, slabs,
    coarse_hbm, fine_hbm, owner_hbm, target_hbm, tags_hbm,
    synced_ref, sums_ref,
    fine, coarse, tags, own_i, tgt_i, meta, rec, chosen, turned, tags_t, total, parts,
    load_sem, msend, mrecv, dsend, drecv, ssend, srecv,
):
    tile_count = coarse.shape[1]
    cells = coarse.shape[2]
    patches = fine.shape[1]
    me = lax.axis_index("blk")
    slab = lax.axis_index("sig")

    def partner(mask):
        index = me
        bit = 1
        while bit <= mask:
            if mask & bit:
                index = index + bit - 2 * bit * ((me // bit) % 2)
            bit *= 2
        return index

    def load(k, src, dst):
        copy = pltpu.make_async_copy(src, dst, load_sem.at[k])
        copy.start()
        return copy

    piece = patches // PIECES
    load_fine = [
        [
            load(f * PIECES + k, fine_hbm.at[pl.ds(k * piece, piece), f], fine.at[f, pl.ds(k * piece, piece)])
            for k in range(PIECES)
        ]
        for f in range(FIELDS)
    ]
    k = FIELDS * PIECES
    load_owner = load(k, owner_hbm, own_i)
    load_target = load(k + 1, target_hbm, tgt_i)
    load_tags = load(k + 2, tags_hbm, tags)
    load_coarse = [load(k + 3 + f, coarse_hbm.at[f], coarse.at[f]) for f in range(FIELDS)]

    barrier = pltpu.get_barrier_semaphore()
    for mask in range(1, blocks):
        pl.semaphore_signal(barrier, inc=1, device_id={"blk": partner(mask)}, device_id_type=MESH)
    for shift in range(1, slabs):
        pl.semaphore_signal(
            barrier, inc=1, device_id={"sig": lax.rem(slab + shift, slabs)}, device_id_type=MESH
        )

    def split(x):
        high = x.astype(jnp.bfloat16)
        return high, (x - high.astype(jnp.float32)).astype(jnp.bfloat16)

    mean = jnp.where(
        lax.broadcasted_iota(jnp.int32, (patches, patches * 8), 1) // 8
        == lax.broadcasted_iota(jnp.int32, (patches, patches * 8), 0),
        0.125, 0.0,
    ).astype(jnp.bfloat16)

    def average(f):
        for copy in load_fine[f]:
            copy.wait()
        high, low = split(fine[f].reshape(patches * 8, cells))
        rows = jnp.dot(mean, high, preferred_element_type=jnp.float32)
        rows = rows + jnp.dot(mean, low, preferred_element_type=jnp.float32)
        rec[0, f] = rows.reshape(rec.shape[2:])

    average(0)
    load_owner.wait()
    load_target.wait()
    code = own_i[...] * tile_count + tgt_i[...]
    wide = jnp.concatenate([code] * (128 // patches), axis=1).astype(jnp.float32)
    meta[0] = jnp.broadcast_to(wide, (8, 128))
    pl.semaphore_wait(barrier, blocks - 1 + slabs - 1)

    started = []

    def send(src, dst, send_sem, recv_sem, device):
        copy = pltpu.make_async_remote_copy(
            src_ref=src, dst_ref=dst, send_sem=send_sem, recv_sem=recv_sem,
            device_id=device, device_id_type=MESH,
        )
        copy.start()
        started.append(copy)
        return copy

    lane = lax.broadcasted_iota(jnp.int32, (1, 4 * patches), 1) // patches
    tile_codes = (
        lax.broadcasted_iota(jnp.int32, (tile_count, 4 * patches), 0) + me * tile_count
    ).astype(jnp.float32)

    def place(slots):
        codes = meta[slots[0]][0:1]
        for k in range(1, 4):
            codes = jnp.where(lane == k, meta[slots[k]][0:1], codes)
        return jnp.where(codes == tile_codes, 1.0, 0.0).astype(jnp.float32)

    def add(chosen, slot, count, f):
        rows = rec[pl.ds(slot, count), f].reshape(count * patches, cells)
        synced_ref[f] += jnp.dot(
            chosen, jnp.concatenate(split(rows), axis=0), preferred_element_type=jnp.float32
        )

    def turn_tags():
        load_tags.wait()
        tags_t[...] = (0.25 * tags[...].astype(jnp.float32)).T.reshape(tags_t.shape)
        total[...] = jnp.zeros_like(total)

    def prepare():
        for copy in metas:
            copy.wait_recv()
        if blocks == 8:
            hits = None
            for k, slots in enumerate(((0, 1, 2, 3), (4, 5, 0, 1), (2, 3, 4, 5), (6, 7, 6, 7))):
                found = place(slots)
                chosen[:, k * 128 : (k + 1) * 128] = found.astype(jnp.bfloat16)
                hits = found if hits is None else jnp.maximum(hits, found)
        else:
            hits = lax.fori_loop(
                0, blocks // 4, lambda k, found: found + place([4 * k, 4 * k + 1, 4 * k + 2, 4 * k + 3]),
                jnp.zeros((tile_count, 4 * patches), jnp.float32),
            )
        free = jnp.max(hits, axis=1, keepdims=True) == 0
        for f in range(FIELDS):
            load_coarse[f].wait()
            synced_ref[f] = jnp.where(free, coarse[f], 0.0)

    depth = lax.broadcasted_iota(jnp.int32, (EDGE, EDGE, tile_count), 1)
    inner_z = (depth > 0) & (depth < EDGE - 1)
    edge_row = jnp.zeros((1, EDGE, tile_count), jnp.float32)

    def weigh(f):
        turned[...] = synced_ref[f].T.reshape(turned.shape)
        for x in range(EDGE):
            mid = turned[x]
            dy = mid[2:] - mid[:-2]
            dz = mid - pltpu.roll(mid, 2, 1)
            value = jnp.where(inner_z, pltpu.roll(dz * dz, EDGE - 1, 1), 0.0)
            value = value + jnp.concatenate([edge_row, dy * dy, edge_row], axis=0)
            if 0 < x < EDGE - 1:
                dx = turned[x + 1] - turned[x - 1]
                value = value + dx * dx
            total[...] += tags_t[x] * value

    metas = []

    def send_metas():
        for mask in range(1, blocks):
            metas.append(
                send(meta.at[0], meta.at[mask], msend.at[mask], mrecv.at[mask], {"blk": partner(mask)})
            )

    if blocks == 8:
        copies = {}

        def go(name, slot, start, count, mask, target, part):
            k = len(copies)
            low, high = part
            fields, halves = pl.ds(low, high - low), pl.ds(start, count)
            copies[name, part] = send(
                rec.at[slot, fields, halves], rec.at[target, fields, halves],
                dsend.at[k], drecv.at[k], {"blk": partner(mask)},
            )

        def came(part, *names):
            for name in names:
                copies[name, part].wait_recv()

        def own(part):
            go("x0", 0, 0, 1, 2, 2, part)
            go("y1", 0, 1, 1, 4, 4, part)
            go("x1", 0, 1, 1, 2, 2, part)
            go("y0", 0, 0, 1, 4, 4, part)

        def forward(part, *pieces):
            for piece in pieces:
                came(piece, "x0")
            go("d0", 2, 0, 1, 4, 6, part)
            for piece in pieces:
                came(piece, "y1")
            go("d1", 4, 1, 1, 2, 6, part)

        def share(part, *pieces):
            for piece in pieces:
                came(piece, "x1")
            go("cx", 2, 0, 2, 1, 3, part)
            for piece in pieces:
                came(piece, "y0")
            go("cy", 4, 0, 2, 1, 5, part)

        def share_diagonal(part):
            came(part, "d0")
            go("cd0", 6, 0, 1, 1, 7, part)
            came(part, "d1")
            go("cd1", 6, 1, 1, 1, 7, part)

        def drain(part, *later):
            kept = [copies[name, part] for name in later if (name, part) in copies]
            for copy in started:
                if not any(copy is other for other in kept):
                    copy.wait_send()
            started[:] = kept

        def add_near(part):
            came(part, "c", "cx", "cy")
            for f in range(*part):
                add(chosen[:, :384], 0, 6, f)

        def add_diagonal(part):
            came(part, "cd0", "cd1")
            for f in range(*part):
                add(chosen[:, 384:], 6, 2, f)

        early, late = (0, FIELDS - 1), (FIELDS - 1, FIELDS)
        pieces = [(f, f + 1) for f in range(FIELDS - 1)]
        own(pieces[0])
        send_metas()
        for piece in pieces[1:]:
            average(piece[0])
            own(piece)
        go("c", 0, 0, 2, 1, 1, early)
        average(FIELDS - 1)
        forward(early, *pieces)
        own(late)
        go("c", 0, 0, 2, 1, 1, late)
        turn_tags()
        share(early, *pieces)
        prepare()
        add_near(early)
        forward(late, late)
        share_diagonal(early)
        share(late, late)
        add_diagonal(early)
        for f in range(*early):
            weigh(f)
        add_near(late)
        drain(late, "d0", "d1")
        share_diagonal(late)
        add_diagonal(late)
        weigh(FIELDS - 1)
    else:
        send_metas()
        for f in range(1, FIELDS):
            average(f)
        bit, k = 1, 0
        while bit < blocks:
            send(
                rec.at[pl.ds(0, bit)], rec.at[pl.ds(bit, bit)], dsend.at[k], drecv.at[k], {"blk": partner(bit)}
            ).wait_recv()
            bit, k = 2 * bit, k + 1
        turn_tags()
        prepare()

        def body(group, carry):
            pair = place([2 * group, 2 * group + 1, 2 * group, 2 * group + 1]).astype(jnp.bfloat16)
            for f in range(FIELDS):
                add(pair, 2 * group, 2, f)
            return carry

        lax.fori_loop(0, blocks // 2, body, 0)
        for f in range(FIELDS):
            weigh(f)

    parts[slab, 0] = jnp.sum(total[...], axis=1)
    parts[slab, 1] = jnp.sum(total[...], axis=0)
    for shift in range(1, slabs):
        send(
            parts.at[slab], parts.at[slab], ssend.at[shift], srecv.at[shift],
            {"sig": lax.rem(slab + shift, slabs)},
        )
    for shift in range(1, slabs):
        source = lax.rem(slab + slabs - shift, slabs)
        pltpu.make_async_remote_copy(
            src_ref=parts.at[source], dst_ref=parts.at[source], send_sem=ssend.at[shift], recv_sem=srecv.at[shift],
            device_id={"sig": lax.rem(slab + shift, slabs)}, device_id_type=MESH,
        ).wait_recv()
    whole = parts[0]
    for k in range(1, slabs):
        whole = whole + parts[k]
    sums_ref[...] = whole

    for copy in started:
        copy.wait_send()


def finish(slabs, synced_in, sums, synced_out, signature, line, sem):
    tile_count = sums.shape[2]
    writes = []
    piece = tile_count // PIECES
    for f in range(FIELDS):
        for k in range(PIECES):
            rows = pl.ds(k * piece, piece)
            writes.append(
                pltpu.make_async_copy(
                    synced_in.at[f, rows], synced_out.at[f, rows], sem.at[1 + f * PIECES + k]
                )
            )
            writes[-1].start()
    along_y = sums[0] * (1.0 / (EDGE * EDGE * slabs))
    along_z = sums[1] * (1.0 / (EDGE * EDGE * tile_count * slabs))
    group = 128 // EDGE
    lines = tile_count // group
    spread = jnp.concatenate([along_y] * group, axis=0)
    row = lax.broadcasted_iota(jnp.int32, (128, tile_count), 0)
    col = lax.broadcasted_iota(jnp.int32, (128, tile_count), 1)
    spread = jnp.where(col % group == row // EDGE, spread, 0.0)
    terms = jnp.concatenate([spread, along_z], axis=0)
    high = terms.astype(jnp.bfloat16).astype(jnp.float32)
    terms = jnp.concatenate([high, terms - high], axis=1).astype(jnp.bfloat16)
    row = lax.broadcasted_iota(jnp.int32, (2 * lines, 2 * tile_count), 0)
    col = lax.broadcasted_iota(jnp.int32, (2 * lines, 2 * tile_count), 1) % tile_count
    pick = jnp.where((col // group == row) | (row >= lines), 1.0, 0.0).astype(jnp.bfloat16)
    order = lax.dot_general(pick, terms, (((1,), (1,)), ((), ())), preferred_element_type=jnp.float32)
    for r in range(lines):
        line[0:1, r * 128 : (r + 1) * 128] = order[r : r + 1, :128]
    line[0:1, lines * 128 : lines * 128 + EDGE] = order[lines : lines + 1, 128:]
    write_line = pltpu.make_async_copy(line, signature, sem.at[0])
    write_line.start()
    for copy in writes:
        copy.wait()
    write_line.wait()


def shards(blocks, slabs, coarse_fields, fine_fields, owner, target_tile, tags):
    tile_count, _, cells = coarse_fields.shape
    patches = fine_fields.shape[0]
    coarse = jnp.transpose(coarse_fields, (1, 0, 2))
    stay = pl.BlockSpec(memory_space=pl.ANY)
    vmem = pl.BlockSpec(memory_space=pltpu.VMEM)
    copies = 26
    f32 = jnp.float32
    synced, sums = pl.pallas_call(
        functools.partial(kernel, blocks, slabs),
        out_shape=(
            jax.ShapeDtypeStruct((FIELDS, tile_count, cells), f32),
            jax.ShapeDtypeStruct((2, EDGE, tile_count), f32),
        ),
        in_specs=[stay] * 5,
        out_specs=(vmem, vmem),
        scratch_shapes=[
            pltpu.VMEM((FIELDS, patches, 8, cells), f32),
            pltpu.VMEM((FIELDS, tile_count, cells), f32),
            pltpu.VMEM((tile_count, cells), jnp.int32),
            pltpu.VMEM((1, patches), jnp.int32),
            pltpu.VMEM((1, patches), jnp.int32),
            pltpu.VMEM((blocks, 8, 128), f32),
            pltpu.VMEM((blocks, FIELDS, 2, patches // 2, cells), f32),
            pltpu.VMEM((tile_count, 512), jnp.bfloat16),
            pltpu.VMEM((EDGE, EDGE, EDGE, tile_count), f32),
            pltpu.VMEM((EDGE, EDGE, EDGE, tile_count), f32),
            pltpu.VMEM((EDGE, EDGE, tile_count), f32),
            pltpu.VMEM((slabs, 2, EDGE, tile_count), f32),
            pltpu.SemaphoreType.DMA((FIELDS * PIECES + 3 + FIELDS,)),
            pltpu.SemaphoreType.DMA((blocks,)),
            pltpu.SemaphoreType.DMA((blocks,)),
            pltpu.SemaphoreType.DMA((copies,)),
            pltpu.SemaphoreType.DMA((copies,)),
            pltpu.SemaphoreType.DMA((slabs,)),
            pltpu.SemaphoreType.DMA((slabs,)),
        ],
        compiler_params=pltpu.CompilerParams(
            collective_id=0, has_side_effects=True, vmem_limit_bytes=VMEM_BYTES
        ),
        name="average_down",
    )(*[
        pltpu.with_memory_space_constraint(x, pltpu.HBM)
        for x in (coarse, fine_fields, owner.reshape(1, patches), target_tile.reshape(1, patches), tags)
    ])
    width = tile_count * EDGE + EDGE
    synced, signature = pl.pallas_call(
        functools.partial(finish, slabs),
        out_shape=(
            jax.ShapeDtypeStruct((FIELDS, tile_count, cells), f32),
            jax.ShapeDtypeStruct((1, width), f32),
        ),
        in_specs=[vmem, vmem],
        out_specs=(stay, stay),
        scratch_shapes=[pltpu.VMEM((1, width), f32), pltpu.SemaphoreType.DMA((1 + FIELDS * PIECES,))],
        compiler_params=pltpu.CompilerParams(vmem_limit_bytes=4 * 1024 * 1024),
        name="write_outputs",
    )(synced, sums)
    return jnp.transpose(synced, (1, 0, 2)), signature


def solution(mesh):
    blocks, slabs = mesh.shape["blk"], mesh.shape["sig"]
    return jax.shard_map(
        functools.partial(shards, blocks, slabs),
        mesh=mesh,
        in_specs=(
            P(("blk", "sig"), None, None),
            P(("blk", "sig"), None, None, None),
            P(("blk", "sig"), None),
            P(("blk", "sig"), None),
            P(("blk", "sig"), None),
        ),
        out_specs=(P(("blk", "sig"), None, None), P("blk", None)),
        check_vma=False,
    )
```

```python
import functools

import jax
import jax.numpy as jnp
from jax import lax
from jax.experimental import pallas as pl
from jax.experimental.pallas import tpu as pltpu
from jax.sharding import PartitionSpec as P

EDGE = 8
FIELDS = 3
PIECES = 4
VMEM_BYTES = 32 * 1024 * 1024
MESH = pl.DeviceIdType.MESH


def kernel(
    blocks, slabs,
    coarse_hbm, fine_hbm, owner_hbm, target_hbm, tags_hbm,
    synced_ref, sums_ref,
    fine, coarse, tags, own_i, tgt_i, meta, rec, chosen, turned, tags_t, total, parts,
    load_sem, msend, mrecv, dsend, drecv, ssend, srecv,
):
    tile_count = coarse.shape[1]
    cells = coarse.shape[2]
    patches = fine.shape[1]
    me = lax.axis_index("blk")
    slab = lax.axis_index("sig")

    def partner(mask):
        index = me
        bit = 1
        while bit <= mask:
            if mask & bit:
                index = index + bit - 2 * bit * ((me // bit) % 2)
            bit *= 2
        return index

    def load(k, src, dst):
        copy = pltpu.make_async_copy(src, dst, load_sem.at[k])
        copy.start()
        return copy

    piece = patches // PIECES
    load_fine = [
        [
            load(f * PIECES + k, fine_hbm.at[pl.ds(k * piece, piece), f], fine.at[f, pl.ds(k * piece, piece)])
            for k in range(PIECES)
        ]
        for f in range(FIELDS)
    ]
    k = FIELDS * PIECES
    load_owner = load(k, owner_hbm, own_i)
    load_target = load(k + 1, target_hbm, tgt_i)
    load_tags = load(k + 2, tags_hbm, tags)
    load_coarse = [load(k + 3 + f, coarse_hbm.at[f], coarse.at[f]) for f in range(FIELDS)]

    barrier = pltpu.get_barrier_semaphore()
    for mask in range(1, blocks):
        pl.semaphore_signal(barrier, inc=1, device_id={"blk": partner(mask)}, device_id_type=MESH)
    for shift in range(1, slabs):
        pl.semaphore_signal(
            barrier, inc=1, device_id={"sig": lax.rem(slab + shift, slabs)}, device_id_type=MESH
        )

    def split(x):
        high = x.astype(jnp.bfloat16)
        return high, (x - high.astype(jnp.float32)).astype(jnp.bfloat16)

    mean = jnp.where(
        lax.broadcasted_iota(jnp.int32, (patches, patches * 8), 1) // 8
        == lax.broadcasted_iota(jnp.int32, (patches, patches * 8), 0),
        0.125, 0.0,
    ).astype(jnp.bfloat16)

    def average(f):
        for copy in load_fine[f]:
            copy.wait()
        high, low = split(fine[f].reshape(patches * 8, cells))
        rows = jnp.dot(mean, high, preferred_element_type=jnp.float32)
        rows = rows + jnp.dot(mean, low, preferred_element_type=jnp.float32)
        rec[0, f] = rows.reshape(rec.shape[2:])

    average(0)
    load_owner.wait()
    load_target.wait()
    code = own_i[...] * tile_count + tgt_i[...]
    wide = jnp.concatenate([code] * (128 // patches), axis=1).astype(jnp.float32)
    meta[0] = jnp.broadcast_to(wide, (8, 128))
    pl.semaphore_wait(barrier, blocks - 1 + slabs - 1)

    started = []

    def send(src, dst, send_sem, recv_sem, device):
        copy = pltpu.make_async_remote_copy(
            src_ref=src, dst_ref=dst, send_sem=send_sem, recv_sem=recv_sem,
            device_id=device, device_id_type=MESH,
        )
        copy.start()
        started.append(copy)
        return copy

    lane = lax.broadcasted_iota(jnp.int32, (1, 4 * patches), 1) // patches
    tile_codes = (
        lax.broadcasted_iota(jnp.int32, (tile_count, 4 * patches), 0) + me * tile_count
    ).astype(jnp.float32)

    def place(slots):
        codes = meta[slots[0]][0:1]
        for k in range(1, 4):
            codes = jnp.where(lane == k, meta[slots[k]][0:1], codes)
        return jnp.where(codes == tile_codes, 1.0, 0.0).astype(jnp.float32)

    def add(chosen, slot, count, f):
        rows = rec[pl.ds(slot, count), f].reshape(count * patches, cells)
        synced_ref[f] += jnp.dot(
            chosen, jnp.concatenate(split(rows), axis=0), preferred_element_type=jnp.float32
        )

    def turn_tags():
        load_tags.wait()
        tags_t[...] = (0.25 * tags[...].astype(jnp.float32)).T.reshape(tags_t.shape)
        total[...] = jnp.zeros_like(total)

    def prepare():
        for copy in metas:
            copy.wait_recv()
        if blocks == 8:
            hits = None
            for k, slots in enumerate(((0, 1, 2, 3), (4, 5, 0, 1), (2, 3, 4, 5), (6, 7, 6, 7))):
                found = place(slots)
                chosen[:, k * 128 : (k + 1) * 128] = found.astype(jnp.bfloat16)
                hits = found if hits is None else jnp.maximum(hits, found)
        else:
            hits = lax.fori_loop(
                0, blocks // 4, lambda k, found: found + place([4 * k, 4 * k + 1, 4 * k + 2, 4 * k + 3]),
                jnp.zeros((tile_count, 4 * patches), jnp.float32),
            )
        free = jnp.max(hits, axis=1, keepdims=True) == 0
        for f in range(FIELDS):
            load_coarse[f].wait()
            synced_ref[f] = jnp.where(free, coarse[f], 0.0)

    depth = lax.broadcasted_iota(jnp.int32, (EDGE, EDGE, tile_count), 1)
    inner_z = (depth > 0) & (depth < EDGE - 1)
    edge_row = jnp.zeros((1, EDGE, tile_count), jnp.float32)

    def weigh(f):
        turned[...] = synced_ref[f].T.reshape(turned.shape)
        for x in range(EDGE):
            mid = turned[x]
            dy = mid[2:] - mid[:-2]
            dz = mid - pltpu.roll(mid, 2, 1)
            value = jnp.where(inner_z, pltpu.roll(dz * dz, EDGE - 1, 1), 0.0)
            value = value + jnp.concatenate([edge_row, dy * dy, edge_row], axis=0)
            if 0 < x < EDGE - 1:
                dx = turned[x + 1] - turned[x - 1]
                value = value + dx * dx
            total[...] += tags_t[x] * value

    metas = []

    def send_metas():
        for mask in range(1, blocks):
            metas.append(
                send(meta.at[0], meta.at[mask], msend.at[mask], mrecv.at[mask], {"blk": partner(mask)})
            )

    if blocks == 8:
        copies = {}

        def go(name, slot, start, count, mask, target, part):
            k = len(copies)
            low, high = part
            fields, halves = pl.ds(low, high - low), pl.ds(start, count)
            copies[name, part] = send(
                rec.at[slot, fields, halves], rec.at[target, fields, halves],
                dsend.at[k], drecv.at[k], {"blk": partner(mask)},
            )

        def came(part, *names):
            for name in names:
                copies[name, part].wait_recv()

        def own(part):
            go("x0", 0, 0, 1, 2, 2, part)
            go("y1", 0, 1, 1, 4, 4, part)
            go("x1", 0, 1, 1, 2, 2, part)
            go("y0", 0, 0, 1, 4, 4, part)

        def forward(part, *pieces):
            for piece in pieces:
                came(piece, "x0")
            go("d0", 2, 0, 1, 4, 6, part)
            for piece in pieces:
                came(piece, "y1")
            go("d1", 4, 1, 1, 2, 6, part)

        def share(part, *pieces):
            for piece in pieces:
                came(piece, "x1")
            go("cx", 2, 0, 2, 1, 3, part)
            for piece in pieces:
                came(piece, "y0")
            go("cy", 4, 0, 2, 1, 5, part)

        def share_diagonal(part):
            came(part, "d0")
            go("cd0", 6, 0, 1, 1, 7, part)
            came(part, "d1")
            go("cd1", 6, 1, 1, 1, 7, part)

        def drain(part, *later):
            kept = [copies[name, part] for name in later if (name, part) in copies]
            for copy in started:
                if not any(copy is other for other in kept):
                    copy.wait_send()
            started[:] = kept

        def add_near(part):
            came(part, "c", "cx", "cy")
            for f in range(*part):
                add(chosen[:, :384], 0, 6, f)

        def add_diagonal(part):
            came(part, "cd0", "cd1")
            for f in range(*part):
                add(chosen[:, 384:], 6, 2, f)

        early, late = (0, FIELDS - 1), (FIELDS - 1, FIELDS)
        pieces = [(f, f + 1) for f in range(FIELDS - 1)]
        own(pieces[0])
        for piece in pieces[1:]:
            average(piece[0])
            own(piece)
        send_metas()
        average(FIELDS - 1)
        own(late)
        go("c", 0, 0, 2, 1, 1, early)
        go("c", 0, 0, 2, 1, 1, late)
        turn_tags()
        forward(early, *pieces)
        share(early, *pieces)
        forward(late, late)
        prepare()
        share(late, late)
        add_near(early)
        share_diagonal(early)
        add_near(late)
        add_diagonal(early)
        drain(late, "d0", "d1")
        share_diagonal(late)
        for f in range(*early):
            weigh(f)
        add_diagonal(late)
        weigh(FIELDS - 1)
    else:
        send_metas()
        for f in range(1, FIELDS):
            average(f)
        bit, k = 1, 0
        while bit < blocks:
            send(
                rec.at[pl.ds(0, bit)], rec.at[pl.ds(bit, bit)], dsend.at[k], drecv.at[k], {"blk": partner(bit)}
            ).wait_recv()
            bit, k = 2 * bit, k + 1
        turn_tags()
        prepare()

        def body(group, carry):
            pair = place([2 * group, 2 * group + 1, 2 * group, 2 * group + 1]).astype(jnp.bfloat16)
            for f in range(FIELDS):
                add(pair, 2 * group, 2, f)
            return carry

        lax.fori_loop(0, blocks // 2, body, 0)
        for f in range(FIELDS):
            weigh(f)

    parts[slab, 0] = jnp.sum(total[...], axis=1)
    parts[slab, 1] = jnp.sum(total[...], axis=0)
    for shift in range(1, slabs):
        send(
            parts.at[slab], parts.at[slab], ssend.at[shift], srecv.at[shift],
            {"sig": lax.rem(slab + shift, slabs)},
        )
    for shift in range(1, slabs):
        source = lax.rem(slab + slabs - shift, slabs)
        pltpu.make_async_remote_copy(
            src_ref=parts.at[source], dst_ref=parts.at[source], send_sem=ssend.at[shift], recv_sem=srecv.at[shift],
            device_id={"sig": lax.rem(slab + shift, slabs)}, device_id_type=MESH,
        ).wait_recv()
    whole = parts[0]
    for k in range(1, slabs):
        whole = whole + parts[k]
    sums_ref[...] = whole

    for copy in started:
        copy.wait_send()


def finish(slabs, synced_in, sums, synced_out, signature, line, sem):
    tile_count = sums.shape[2]
    writes = []
    piece = tile_count // PIECES
    for f in range(FIELDS):
        for k in range(PIECES):
            rows = pl.ds(k * piece, piece)
            writes.append(
                pltpu.make_async_copy(
                    synced_in.at[f, rows], synced_out.at[f, rows], sem.at[1 + f * PIECES + k]
                )
            )
            writes[-1].start()
    along_y = sums[0] * (1.0 / (EDGE * EDGE * slabs))
    along_z = sums[1] * (1.0 / (EDGE * EDGE * tile_count * slabs))
    group = 128 // EDGE
    lines = tile_count // group
    spread = jnp.concatenate([along_y] * group, axis=0)
    row = lax.broadcasted_iota(jnp.int32, (128, tile_count), 0)
    col = lax.broadcasted_iota(jnp.int32, (128, tile_count), 1)
    spread = jnp.where(col % group == row // EDGE, spread, 0.0)
    terms = jnp.concatenate([spread, along_z], axis=0)
    high = terms.astype(jnp.bfloat16).astype(jnp.float32)
    terms = jnp.concatenate([high, terms - high], axis=1).astype(jnp.bfloat16)
    row = lax.broadcasted_iota(jnp.int32, (2 * lines, 2 * tile_count), 0)
    col = lax.broadcasted_iota(jnp.int32, (2 * lines, 2 * tile_count), 1) % tile_count
    pick = jnp.where((col // group == row) | (row >= lines), 1.0, 0.0).astype(jnp.bfloat16)
    order = lax.dot_general(pick, terms, (((1,), (1,)), ((), ())), preferred_element_type=jnp.float32)
    for r in range(lines):
        line[0:1, r * 128 : (r + 1) * 128] = order[r : r + 1, :128]
    line[0:1, lines * 128 : lines * 128 + EDGE] = order[lines : lines + 1, 128:]
    write_line = pltpu.make_async_copy(line, signature, sem.at[0])
    write_line.start()
    for copy in writes:
        copy.wait()
    write_line.wait()


def shards(blocks, slabs, coarse_fields, fine_fields, owner, target_tile, tags):
    tile_count, _, cells = coarse_fields.shape
    patches = fine_fields.shape[0]
    coarse = jnp.transpose(coarse_fields, (1, 0, 2))
    stay = pl.BlockSpec(memory_space=pl.ANY)
    vmem = pl.BlockSpec(memory_space=pltpu.VMEM)
    copies = 26
    f32 = jnp.float32
    synced, sums = pl.pallas_call(
        functools.partial(kernel, blocks, slabs),
        out_shape=(
            jax.ShapeDtypeStruct((FIELDS, tile_count, cells), f32),
            jax.ShapeDtypeStruct((2, EDGE, tile_count), f32),
        ),
        in_specs=[stay] * 5,
        out_specs=(vmem, vmem),
        scratch_shapes=[
            pltpu.VMEM((FIELDS, patches, 8, cells), f32),
            pltpu.VMEM((FIELDS, tile_count, cells), f32),
            pltpu.VMEM((tile_count, cells), jnp.int32),
            pltpu.VMEM((1, patches), jnp.int32),
            pltpu.VMEM((1, patches), jnp.int32),
            pltpu.VMEM((blocks, 8, 128), f32),
            pltpu.VMEM((blocks, FIELDS, 2, patches // 2, cells), f32),
            pltpu.VMEM((tile_count, 512), jnp.bfloat16),
            pltpu.VMEM((EDGE, EDGE, EDGE, tile_count), f32),
            pltpu.VMEM((EDGE, EDGE, EDGE, tile_count), f32),
            pltpu.VMEM((EDGE, EDGE, tile_count), f32),
            pltpu.VMEM((slabs, 2, EDGE, tile_count), f32),
            pltpu.SemaphoreType.DMA((FIELDS * PIECES + 3 + FIELDS,)),
            pltpu.SemaphoreType.DMA((blocks,)),
            pltpu.SemaphoreType.DMA((blocks,)),
            pltpu.SemaphoreType.DMA((copies,)),
            pltpu.SemaphoreType.DMA((copies,)),
            pltpu.SemaphoreType.DMA((slabs,)),
            pltpu.SemaphoreType.DMA((slabs,)),
        ],
        compiler_params=pltpu.CompilerParams(
            collective_id=0, has_side_effects=True, vmem_limit_bytes=VMEM_BYTES
        ),
        name="average_down",
    )(*[
        pltpu.with_memory_space_constraint(x, pltpu.HBM)
        for x in (coarse, fine_fields, owner.reshape(1, patches), target_tile.reshape(1, patches), tags)
    ])
    width = tile_count * EDGE + EDGE
    synced, signature = pl.pallas_call(
        functools.partial(finish, slabs),
        out_shape=(
            jax.ShapeDtypeStruct((FIELDS, tile_count, cells), f32),
            jax.ShapeDtypeStruct((1, width), f32),
        ),
        in_specs=[vmem, vmem],
        out_specs=(stay, stay),
        scratch_shapes=[pltpu.VMEM((1, width), f32), pltpu.SemaphoreType.DMA((1 + FIELDS * PIECES,))],
        compiler_params=pltpu.CompilerParams(vmem_limit_bytes=4 * 1024 * 1024),
        name="write_outputs",
    )(synced, sums)
    return jnp.transpose(synced, (1, 0, 2)), signature


def solution(mesh):
    blocks, slabs = mesh.shape["blk"], mesh.shape["sig"]
    return jax.shard_map(
        functools.partial(shards, blocks, slabs),
        mesh=mesh,
        in_specs=(
            P(("blk", "sig"), None, None),
            P(("blk", "sig"), None, None, None),
            P(("blk", "sig"), None),
            P(("blk", "sig"), None),
            P(("blk", "sig"), None),
        ),
        out_specs=(P(("blk", "sig"), None, None), P("blk", None)),
        check_vma=False,
    )
```

```python
import functools

import jax
import jax.numpy as jnp
from jax import lax
from jax.experimental import pallas as pl
from jax.experimental.pallas import tpu as pltpu
from jax.sharding import PartitionSpec as P

EDGE = 8
FIELDS = 3
PIECES = 4
VMEM_BYTES = 32 * 1024 * 1024
MESH = pl.DeviceIdType.MESH


def kernel(
    blocks, slabs,
    coarse_hbm, fine_hbm, owner_hbm, target_hbm, tags_hbm,
    synced_ref, sums_ref,
    fine, coarse, tags, own_i, tgt_i, meta, rec, chosen, turned, tags_t, total, parts,
    load_sem, msend, mrecv, dsend, drecv, ssend, srecv,
):
    tile_count = coarse.shape[1]
    cells = coarse.shape[2]
    patches = fine.shape[1]
    me = lax.axis_index("blk")
    slab = lax.axis_index("sig")

    def partner(mask):
        index = me
        bit = 1
        while bit <= mask:
            if mask & bit:
                index = index + bit - 2 * bit * ((me // bit) % 2)
            bit *= 2
        return index

    def load(k, src, dst):
        copy = pltpu.make_async_copy(src, dst, load_sem.at[k])
        copy.start()
        return copy

    load_fine = [load(f, fine_hbm.at[:, f], fine.at[f]) for f in range(FIELDS - 1)]

    barrier = pltpu.get_barrier_semaphore()
    for mask in range(1, blocks):
        pl.semaphore_signal(barrier, inc=1, device_id={"blk": partner(mask)}, device_id_type=MESH)
    for shift in range(1, slabs):
        pl.semaphore_signal(
            barrier, inc=1, device_id={"sig": lax.rem(slab + shift, slabs)}, device_id_type=MESH
        )

    load_owner = load(FIELDS, owner_hbm, own_i)
    load_target = load(FIELDS + 1, target_hbm, tgt_i)
    load_fine.append(load(FIELDS - 1, fine_hbm.at[:, FIELDS - 1], fine.at[FIELDS - 1]))
    load_tags = load(FIELDS + 2, tags_hbm, tags)
    load_coarse = load(FIELDS + 3, coarse_hbm, coarse)

    def split(x):
        high = x.astype(jnp.bfloat16)
        return high, (x - high.astype(jnp.float32)).astype(jnp.bfloat16)

    mean = jnp.where(
        lax.broadcasted_iota(jnp.int32, (patches, patches * 8), 1) // 8
        == lax.broadcasted_iota(jnp.int32, (patches, patches * 8), 0),
        0.125, 0.0,
    ).astype(jnp.bfloat16)

    def average(f):
        load_fine[f].wait()
        high, low = split(fine[f].reshape(patches * 8, cells))
        rows = jnp.dot(mean, high, preferred_element_type=jnp.float32)
        rows = rows + jnp.dot(mean, low, preferred_element_type=jnp.float32)
        rec[0, f] = rows.reshape(rec.shape[2:])

    for f in range(FIELDS - 1):
        average(f)
    load_owner.wait()
    load_target.wait()
    code = own_i[...] * tile_count + tgt_i[...]
    wide = jnp.concatenate([code] * (128 // patches), axis=1).astype(jnp.float32)
    meta[0] = jnp.broadcast_to(wide, (8, 128))
    pl.semaphore_wait(barrier, blocks - 1 + slabs - 1)

    started = []

    def send(src, dst, send_sem, recv_sem, device):
        copy = pltpu.make_async_remote_copy(
            src_ref=src, dst_ref=dst, send_sem=send_sem, recv_sem=recv_sem,
            device_id=device, device_id_type=MESH,
        )
        copy.start()
        started.append(copy)
        return copy

    lane = lax.broadcasted_iota(jnp.int32, (1, 4 * patches), 1) // patches
    tile_codes = (
        lax.broadcasted_iota(jnp.int32, (tile_count, 4 * patches), 0) + me * tile_count
    ).astype(jnp.float32)

    def place(slots):
        codes = meta[slots[0]][0:1]
        for k in range(1, 4):
            codes = jnp.where(lane == k, meta[slots[k]][0:1], codes)
        return jnp.where(codes == tile_codes, 1.0, 0.0).astype(jnp.float32)

    def add(chosen, slot, count, f):
        rows = rec[pl.ds(slot, count), f].reshape(count * patches, cells)
        synced_ref[f] += jnp.dot(
            chosen, jnp.concatenate(split(rows), axis=0), preferred_element_type=jnp.float32
        )

    def turn_tags():
        load_tags.wait()
        tags_t[...] = (0.25 * tags[...].astype(jnp.float32)).T.reshape(tags_t.shape)
        total[...] = jnp.zeros_like(total)

    def prepare():
        for copy in metas:
            copy.wait_recv()
        if blocks == 8:
            hits = None
            for k, slots in enumerate(((0, 1, 2, 3), (4, 5, 0, 1), (2, 3, 4, 5), (6, 7, 6, 7))):
                found = place(slots)
                chosen[:, k * 128 : (k + 1) * 128] = found.astype(jnp.bfloat16)
                hits = found if hits is None else jnp.maximum(hits, found)
        else:
            hits = lax.fori_loop(
                0, blocks // 4, lambda k, found: found + place([4 * k, 4 * k + 1, 4 * k + 2, 4 * k + 3]),
                jnp.zeros((tile_count, 4 * patches), jnp.float32),
            )
        free = jnp.max(hits, axis=1, keepdims=True) == 0
        load_coarse.wait()
        for f in range(FIELDS):
            synced_ref[f] = jnp.where(free, coarse[f], 0.0)

    depth = lax.broadcasted_iota(jnp.int32, (EDGE, EDGE, tile_count), 1)
    inner_z = (depth > 0) & (depth < EDGE - 1)
    edge_row = jnp.zeros((1, EDGE, tile_count), jnp.float32)

    def weigh(f):
        turned[...] = synced_ref[f].T.reshape(turned.shape)
        for x in range(EDGE):
            mid = turned[x]
            dy = mid[2:] - mid[:-2]
            dz = mid - pltpu.roll(mid, 2, 1)
            value = jnp.where(inner_z, pltpu.roll(dz * dz, EDGE - 1, 1), 0.0)
            value = value + jnp.concatenate([edge_row, dy * dy, edge_row], axis=0)
            if 0 < x < EDGE - 1:
                dx = turned[x + 1] - turned[x - 1]
                value = value + dx * dx
            total[...] += tags_t[x] * value

    metas = []

    def send_metas():
        for mask in range(1, blocks):
            metas.append(
                send(meta.at[0], meta.at[mask], msend.at[mask], mrecv.at[mask], {"blk": partner(mask)})
            )

    if blocks == 8:
        copies = {}
        early, late = (0, FIELDS - 1), (FIELDS - 1, FIELDS)

        def go(name, slot, start, count, mask, target, part):
            k = len(copies)
            low, high = part
            fields, halves = pl.ds(low, high - low), pl.ds(start, count)
            copies[name, part] = send(
                rec.at[slot, fields, halves], rec.at[target, fields, halves],
                dsend.at[k], drecv.at[k], {"blk": partner(mask)},
            )

        def came(part, *names):
            for name in names:
                copies[name, part].wait_recv()

        def own(part):
            go("x0", 0, 0, 1, 2, 2, part)
            go("y1", 0, 1, 1, 4, 4, part)
            go("x1", 0, 1, 1, 2, 2, part)
            go("y0", 0, 0, 1, 4, 4, part)
            go("c", 0, 0, 2, 1, 1, part)

        def forward(part):
            came(part, "x0")
            go("d0", 2, 0, 1, 4, 6, part)
            came(part, "y1")
            go("d1", 4, 1, 1, 2, 6, part)

        def share(part):
            came(part, "x1")
            go("cx", 2, 0, 2, 1, 3, part)
            came(part, "y0")
            go("cy", 4, 0, 2, 1, 5, part)

        def share_diagonal(part):
            came(part, "d0")
            if part == late:
                go("cd0", 6, 0, 1, 1, 7, part)
            came(part, "d1")
            if part == late:
                go("cd1", 6, 1, 1, 1, 7, part)
            else:
                go("cd", 6, 0, 2, 1, 7, part)

        def drain(part, *later):
            kept = [copies[name, part] for name in later if (name, part) in copies]
            for copy in started:
                if not any(copy is other for other in kept):
                    copy.wait_send()
            started[:] = kept

        def add_near(part):
            came(part, "c", "cx", "cy")
            for f in range(*part):
                add(chosen[:, :384], 0, 6, f)

        def add_diagonal(part):
            came(part, *(("cd0", "cd1") if part == late else ("cd",)))
            for f in range(*part):
                add(chosen[:, 384:], 6, 2, f)

        own(early)
        send_metas()
        average(FIELDS - 1)
        own(late)
        turn_tags()
        forward(early)
        share(early)
        forward(late)
        prepare()
        share(late)
        add_near(early)
        share_diagonal(early)
        add_near(late)
        add_diagonal(early)
        drain(late, "d0", "d1")
        share_diagonal(late)
        for f in range(*early):
            weigh(f)
        add_diagonal(late)
        weigh(FIELDS - 1)
    else:
        send_metas()
        average(FIELDS - 1)
        bit, k = 1, 0
        while bit < blocks:
            send(
                rec.at[pl.ds(0, bit)], rec.at[pl.ds(bit, bit)], dsend.at[k], drecv.at[k], {"blk": partner(bit)}
            ).wait_recv()
            bit, k = 2 * bit, k + 1
        turn_tags()
        prepare()

        def body(group, carry):
            pair = place([2 * group, 2 * group + 1, 2 * group, 2 * group + 1]).astype(jnp.bfloat16)
            for f in range(FIELDS):
                add(pair, 2 * group, 2, f)
            return carry

        lax.fori_loop(0, blocks // 2, body, 0)
        for f in range(FIELDS):
            weigh(f)

    parts[slab, 0] = jnp.sum(total[...], axis=1)
    parts[slab, 1] = jnp.sum(total[...], axis=0)
    for shift in range(1, slabs):
        send(
            parts.at[slab], parts.at[slab], ssend.at[shift], srecv.at[shift],
            {"sig": lax.rem(slab + shift, slabs)},
        )
    for shift in range(1, slabs):
        source = lax.rem(slab + slabs - shift, slabs)
        pltpu.make_async_remote_copy(
            src_ref=parts.at[source], dst_ref=parts.at[source], send_sem=ssend.at[shift], recv_sem=srecv.at[shift],
            device_id={"sig": lax.rem(slab + shift, slabs)}, device_id_type=MESH,
        ).wait_recv()
    whole = parts[0]
    for k in range(1, slabs):
        whole = whole + parts[k]
    sums_ref[...] = whole

    for copy in started:
        copy.wait_send()


def finish(slabs, synced_in, sums, synced_out, signature, line, sem):
    tile_count = sums.shape[2]
    writes = []
    piece = tile_count // PIECES
    for f in range(FIELDS):
        for k in range(PIECES):
            rows = pl.ds(k * piece, piece)
            writes.append(
                pltpu.make_async_copy(
                    synced_in.at[f, rows], synced_out.at[f, rows], sem.at[1 + f * PIECES + k]
                )
            )
            writes[-1].start()
    along_y = sums[0] * (1.0 / (EDGE * EDGE * slabs))
    along_z = sums[1] * (1.0 / (EDGE * EDGE * tile_count * slabs))
    group = 128 // EDGE
    lines = tile_count // group
    spread = jnp.concatenate([along_y] * group, axis=0)
    row = lax.broadcasted_iota(jnp.int32, (128, tile_count), 0)
    col = lax.broadcasted_iota(jnp.int32, (128, tile_count), 1)
    spread = jnp.where(col % group == row // EDGE, spread, 0.0)
    terms = jnp.concatenate([spread, along_z], axis=0)
    high = terms.astype(jnp.bfloat16).astype(jnp.float32)
    terms = jnp.concatenate([high, terms - high], axis=1).astype(jnp.bfloat16)
    row = lax.broadcasted_iota(jnp.int32, (2 * lines, 2 * tile_count), 0)
    col = lax.broadcasted_iota(jnp.int32, (2 * lines, 2 * tile_count), 1) % tile_count
    pick = jnp.where((col // group == row) | (row >= lines), 1.0, 0.0).astype(jnp.bfloat16)
    order = lax.dot_general(pick, terms, (((1,), (1,)), ((), ())), preferred_element_type=jnp.float32)
    for r in range(lines):
        line[0:1, r * 128 : (r + 1) * 128] = order[r : r + 1, :128]
    line[0:1, lines * 128 : lines * 128 + EDGE] = order[lines : lines + 1, 128:]
    write_line = pltpu.make_async_copy(line, signature, sem.at[0])
    write_line.start()
    for copy in writes:
        copy.wait()
    write_line.wait()


def shards(blocks, slabs, coarse_fields, fine_fields, owner, target_tile, tags):
    tile_count, _, cells = coarse_fields.shape
    patches = fine_fields.shape[0]
    coarse = jnp.transpose(coarse_fields, (1, 0, 2))
    stay = pl.BlockSpec(memory_space=pl.ANY)
    vmem = pl.BlockSpec(memory_space=pltpu.VMEM)
    copies = 21
    f32 = jnp.float32
    synced, sums = pl.pallas_call(
        functools.partial(kernel, blocks, slabs),
        out_shape=(
            jax.ShapeDtypeStruct((FIELDS, tile_count, cells), f32),
            jax.ShapeDtypeStruct((2, EDGE, tile_count), f32),
        ),
        in_specs=[stay] * 5,
        out_specs=(vmem, vmem),
        scratch_shapes=[
            pltpu.VMEM((FIELDS, patches, 8, cells), f32),
            pltpu.VMEM((FIELDS, tile_count, cells), f32),
            pltpu.VMEM((tile_count, cells), jnp.int32),
            pltpu.VMEM((1, patches), jnp.int32),
            pltpu.VMEM((1, patches), jnp.int32),
            pltpu.VMEM((blocks, 8, 128), f32),
            pltpu.VMEM((blocks, FIELDS, 2, patches // 2, cells), f32),
            pltpu.VMEM((tile_count, 512), jnp.bfloat16),
            pltpu.VMEM((EDGE, EDGE, EDGE, tile_count), f32),
            pltpu.VMEM((EDGE, EDGE, EDGE, tile_count), f32),
            pltpu.VMEM((EDGE, EDGE, tile_count), f32),
            pltpu.VMEM((slabs, 2, EDGE, tile_count), f32),
            pltpu.SemaphoreType.DMA((FIELDS + 4,)),
            pltpu.SemaphoreType.DMA((blocks,)),
            pltpu.SemaphoreType.DMA((blocks,)),
            pltpu.SemaphoreType.DMA((copies,)),
            pltpu.SemaphoreType.DMA((copies,)),
            pltpu.SemaphoreType.DMA((slabs,)),
            pltpu.SemaphoreType.DMA((slabs,)),
        ],
        compiler_params=pltpu.CompilerParams(
            collective_id=0, has_side_effects=True, vmem_limit_bytes=VMEM_BYTES
        ),
        name="average_down",
    )(*[
        pltpu.with_memory_space_constraint(x, pltpu.HBM)
        for x in (coarse, fine_fields, owner.reshape(1, patches), target_tile.reshape(1, patches), tags)
    ])
    width = tile_count * EDGE + EDGE
    synced, signature = pl.pallas_call(
        functools.partial(finish, slabs),
        out_shape=(
            jax.ShapeDtypeStruct((FIELDS, tile_count, cells), f32),
            jax.ShapeDtypeStruct((1, width), f32),
        ),
        in_specs=[vmem, vmem],
        out_specs=(stay, stay),
        scratch_shapes=[pltpu.VMEM((1, width), f32), pltpu.SemaphoreType.DMA((1 + FIELDS * PIECES,))],
        compiler_params=pltpu.CompilerParams(vmem_limit_bytes=4 * 1024 * 1024),
        name="write_outputs",
    )(synced, sums)
    return jnp.transpose(synced, (1, 0, 2)), signature


def solution(mesh):
    blocks, slabs = mesh.shape["blk"], mesh.shape["sig"]
    return jax.shard_map(
        functools.partial(shards, blocks, slabs),
        mesh=mesh,
        in_specs=(
            P(("blk", "sig"), None, None),
            P(("blk", "sig"), None, None, None),
            P(("blk", "sig"), None),
            P(("blk", "sig"), None),
            P(("blk", "sig"), None),
        ),
        out_specs=(P(("blk", "sig"), None, None), P("blk", None)),
        check_vma=False,
    )
```

```python
import functools

import jax
import jax.numpy as jnp
from jax import lax
from jax.experimental import pallas as pl
from jax.experimental.pallas import tpu as pltpu
from jax.sharding import PartitionSpec as P

EDGE = 8
FIELDS = 3
PIECES = 4
VMEM_BYTES = 32 * 1024 * 1024
MESH = pl.DeviceIdType.MESH


def kernel(
    blocks, slabs,
    coarse_hbm, fine_hbm, owner_hbm, target_hbm, tags_hbm,
    synced_ref, sums_ref,
    fine, coarse, tags, own_i, tgt_i, meta, rec, chosen, turned, tags_t, total, parts,
    load_sem, msend, mrecv, dsend, drecv, ssend, srecv,
):
    tile_count = coarse.shape[1]
    cells = coarse.shape[2]
    patches = fine.shape[1]
    me = lax.axis_index("blk")
    slab = lax.axis_index("sig")

    def partner(mask):
        index = me
        bit = 1
        while bit <= mask:
            if mask & bit:
                index = index + bit - 2 * bit * ((me // bit) % 2)
            bit *= 2
        return index

    def load(k, src, dst):
        copy = pltpu.make_async_copy(src, dst, load_sem.at[k])
        copy.start()
        return copy

    load_fine = [load(f, fine_hbm.at[:, f], fine.at[f]) for f in range(FIELDS - 1)]

    barrier = pltpu.get_barrier_semaphore()
    for mask in range(1, blocks):
        pl.semaphore_signal(barrier, inc=1, device_id={"blk": partner(mask)}, device_id_type=MESH)
    for shift in range(1, slabs):
        pl.semaphore_signal(
            barrier, inc=1, device_id={"sig": lax.rem(slab + shift, slabs)}, device_id_type=MESH
        )

    load_owner = load(FIELDS, owner_hbm, own_i)
    load_target = load(FIELDS + 1, target_hbm, tgt_i)
    load_fine.append(load(FIELDS - 1, fine_hbm.at[:, FIELDS - 1], fine.at[FIELDS - 1]))
    load_tags = load(FIELDS + 2, tags_hbm, tags)
    load_coarse = load(FIELDS + 3, coarse_hbm, coarse)

    def split(x):
        high = x.astype(jnp.bfloat16)
        return high, (x - high.astype(jnp.float32)).astype(jnp.bfloat16)

    mean = jnp.where(
        lax.broadcasted_iota(jnp.int32, (patches, patches * 8), 1) // 8
        == lax.broadcasted_iota(jnp.int32, (patches, patches * 8), 0),
        0.125, 0.0,
    ).astype(jnp.bfloat16)

    def average(f):
        load_fine[f].wait()
        high, low = split(fine[f].reshape(patches * 8, cells))
        rows = jnp.dot(mean, high, preferred_element_type=jnp.float32)
        rows = rows + jnp.dot(mean, low, preferred_element_type=jnp.float32)
        rec[0, f] = rows.reshape(rec.shape[2:])

    for f in range(FIELDS - 1):
        average(f)
    load_owner.wait()
    load_target.wait()
    code = own_i[...] * tile_count + tgt_i[...]
    wide = jnp.concatenate([code] * (128 // patches), axis=1).astype(jnp.float32)
    meta[0] = jnp.broadcast_to(wide, (8, 128))
    pl.semaphore_wait(barrier, blocks - 1 + slabs - 1)

    started = []

    def send(src, dst, send_sem, recv_sem, device):
        copy = pltpu.make_async_remote_copy(
            src_ref=src, dst_ref=dst, send_sem=send_sem, recv_sem=recv_sem,
            device_id=device, device_id_type=MESH,
        )
        copy.start()
        started.append(copy)
        return copy

    lane = lax.broadcasted_iota(jnp.int32, (1, 4 * patches), 1) // patches
    tile_codes = (
        lax.broadcasted_iota(jnp.int32, (tile_count, 4 * patches), 0) + me * tile_count
    ).astype(jnp.float32)

    def place(slots):
        codes = meta[slots[0]][0:1]
        for k in range(1, 4):
            codes = jnp.where(lane == k, meta[slots[k]][0:1], codes)
        return jnp.where(codes == tile_codes, 1.0, 0.0).astype(jnp.float32)

    def add(chosen, slot, count, f):
        rows = rec[pl.ds(slot, count), f].reshape(count * patches, cells)
        synced_ref[f] += jnp.dot(
            chosen, jnp.concatenate(split(rows), axis=0), preferred_element_type=jnp.float32
        )

    def turn_tags():
        load_tags.wait()
        tags_t[...] = (0.25 * tags[...].astype(jnp.float32)).T.reshape(tags_t.shape)
        total[...] = jnp.zeros_like(total)

    def prepare():
        for copy in metas:
            copy.wait_recv()
        if blocks == 8:
            hits = None
            for k, slots in enumerate(((0, 1, 2, 3), (4, 5, 0, 1), (2, 3, 4, 5), (6, 7, 6, 7))):
                found = place(slots)
                chosen[:, k * 128 : (k + 1) * 128] = found.astype(jnp.bfloat16)
                hits = found if hits is None else jnp.maximum(hits, found)
        else:
            hits = lax.fori_loop(
                0, blocks // 4, lambda k, found: found + place([4 * k, 4 * k + 1, 4 * k + 2, 4 * k + 3]),
                jnp.zeros((tile_count, 4 * patches), jnp.float32),
            )
        free = jnp.max(hits, axis=1, keepdims=True) == 0
        load_coarse.wait()
        for f in range(FIELDS):
            synced_ref[f] = jnp.where(free, coarse[f], 0.0)

    depth = lax.broadcasted_iota(jnp.int32, (EDGE, EDGE, tile_count), 1)
    inner_z = (depth > 0) & (depth < EDGE - 1)
    edge_row = jnp.zeros((1, EDGE, tile_count), jnp.float32)

    def weigh(f):
        turned[...] = synced_ref[f].T.reshape(turned.shape)
        for x in range(EDGE):
            mid = turned[x]
            dy = mid[2:] - mid[:-2]
            dz = mid - pltpu.roll(mid, 2, 1)
            value = jnp.where(inner_z, pltpu.roll(dz * dz, EDGE - 1, 1), 0.0)
            value = value + jnp.concatenate([edge_row, dy * dy, edge_row], axis=0)
            if 0 < x < EDGE - 1:
                dx = turned[x + 1] - turned[x - 1]
                value = value + dx * dx
            total[...] += tags_t[x] * value

    metas = []

    def send_metas():
        for mask in range(1, blocks):
            metas.append(
                send(meta.at[0], meta.at[mask], msend.at[mask], mrecv.at[mask], {"blk": partner(mask)})
            )

    if blocks == 8:
        copies = {}
        early, late = (0, FIELDS - 1), (FIELDS - 1, FIELDS)

        def go(name, slot, start, count, mask, target, part):
            k = len(copies)
            low, high = part
            fields, halves = pl.ds(low, high - low), pl.ds(start, count)
            copies[name, part] = send(
                rec.at[slot, fields, halves], rec.at[target, fields, halves],
                dsend.at[k], drecv.at[k], {"blk": partner(mask)},
            )

        def came(part, *names):
            for name in names:
                copies[name, part].wait_recv()

        def own(part):
            go("x0", 0, 0, 1, 2, 2, part)
            go("y1", 0, 1, 1, 4, 4, part)
            go("x1", 0, 1, 1, 2, 2, part)
            go("y0", 0, 0, 1, 4, 4, part)
            go("c", 0, 0, 2, 1, 1, part)

        def forward(part):
            came(part, "x0")
            go("d0", 2, 0, 1, 4, 6, part)
            came(part, "y1")
            go("d1", 4, 1, 1, 2, 6, part)

        def share(part):
            came(part, "x1")
            go("cx", 2, 0, 2, 1, 3, part)
            came(part, "y0")
            go("cy", 4, 0, 2, 1, 5, part)

        def share_diagonal(part):
            came(part, "d0")
            if part == late:
                go("cd0", 6, 0, 1, 1, 7, part)
            came(part, "d1")
            if part == late:
                go("cd1", 6, 1, 1, 1, 7, part)
            else:
                go("cd", 6, 0, 2, 1, 7, part)

        def drain(*kept):
            for copy in started:
                if not any(copy is other for other in kept):
                    copy.wait_send()
            started[:] = kept

        def add_near(part):
            came(part, "c", "cx", "cy")
            for f in range(*part):
                add(chosen[:, :384], 0, 6, f)

        def add_diagonal(part):
            came(part, *(("cd0", "cd1") if part == late else ("cd",)))
            for f in range(*part):
                add(chosen[:, 384:], 6, 2, f)

        own(early)
        send_metas()
        average(FIELDS - 1)
        own(late)
        turn_tags()
        forward(early)
        share(early)
        forward(late)
        prepare()
        share(late)
        add_near(early)
        share_diagonal(early)
        add_near(late)
        drain(copies["cd", early], copies["d0", late], copies["d1", late])
        share_diagonal(late)
        add_diagonal(early)
        for f in range(*early):
            weigh(f)
        add_diagonal(late)
        weigh(FIELDS - 1)
    else:
        send_metas()
        average(FIELDS - 1)
        bit, k = 1, 0
        while bit < blocks:
            send(
                rec.at[pl.ds(0, bit)], rec.at[pl.ds(bit, bit)], dsend.at[k], drecv.at[k], {"blk": partner(bit)}
            ).wait_recv()
            bit, k = 2 * bit, k + 1
        turn_tags()
        prepare()

        def body(group, carry):
            pair = place([2 * group, 2 * group + 1, 2 * group, 2 * group + 1]).astype(jnp.bfloat16)
            for f in range(FIELDS):
                add(pair, 2 * group, 2, f)
            return carry

        lax.fori_loop(0, blocks // 2, body, 0)
        for f in range(FIELDS):
            weigh(f)

    parts[slab, 0] = jnp.sum(total[...], axis=1)
    parts[slab, 1] = jnp.sum(total[...], axis=0)
    for shift in range(1, slabs):
        send(
            parts.at[slab], parts.at[slab], ssend.at[shift], srecv.at[shift],
            {"sig": lax.rem(slab + shift, slabs)},
        )
    for shift in range(1, slabs):
        source = lax.rem(slab + slabs - shift, slabs)
        pltpu.make_async_remote_copy(
            src_ref=parts.at[source], dst_ref=parts.at[source], send_sem=ssend.at[shift], recv_sem=srecv.at[shift],
            device_id={"sig": lax.rem(slab + shift, slabs)}, device_id_type=MESH,
        ).wait_recv()
    whole = parts[0]
    for k in range(1, slabs):
        whole = whole + parts[k]
    sums_ref[...] = whole

    for copy in started:
        copy.wait_send()


def finish(slabs, synced_in, sums, synced_out, signature, line, sem):
    tile_count = sums.shape[2]
    writes = []
    piece = tile_count // PIECES
    for f in range(FIELDS):
        for k in range(PIECES):
            rows = pl.ds(k * piece, piece)
            writes.append(
                pltpu.make_async_copy(
                    synced_in.at[f, rows], synced_out.at[f, rows], sem.at[1 + f * PIECES + k]
                )
            )
            writes[-1].start()
    along_y = sums[0] * (1.0 / (EDGE * EDGE * slabs))
    along_z = sums[1] * (1.0 / (EDGE * EDGE * tile_count * slabs))
    group = 128 // EDGE
    lines = tile_count // group
    spread = jnp.concatenate([along_y] * group, axis=0)
    row = lax.broadcasted_iota(jnp.int32, (128, tile_count), 0)
    col = lax.broadcasted_iota(jnp.int32, (128, tile_count), 1)
    spread = jnp.where(col % group == row // EDGE, spread, 0.0)
    terms = jnp.concatenate([spread, along_z], axis=0)
    high = terms.astype(jnp.bfloat16).astype(jnp.float32)
    terms = jnp.concatenate([high, terms - high], axis=1).astype(jnp.bfloat16)
    row = lax.broadcasted_iota(jnp.int32, (2 * lines, 2 * tile_count), 0)
    col = lax.broadcasted_iota(jnp.int32, (2 * lines, 2 * tile_count), 1) % tile_count
    pick = jnp.where((col // group == row) | (row >= lines), 1.0, 0.0).astype(jnp.bfloat16)
    order = lax.dot_general(pick, terms, (((1,), (1,)), ((), ())), preferred_element_type=jnp.float32)
    for r in range(lines):
        line[0:1, r * 128 : (r + 1) * 128] = order[r : r + 1, :128]
    line[0:1, lines * 128 : lines * 128 + EDGE] = order[lines : lines + 1, 128:]
    write_line = pltpu.make_async_copy(line, signature, sem.at[0])
    write_line.start()
    for copy in writes:
        copy.wait()
    write_line.wait()


def shards(blocks, slabs, coarse_fields, fine_fields, owner, target_tile, tags):
    tile_count, _, cells = coarse_fields.shape
    patches = fine_fields.shape[0]
    coarse = jnp.transpose(coarse_fields, (1, 0, 2))
    stay = pl.BlockSpec(memory_space=pl.ANY)
    vmem = pl.BlockSpec(memory_space=pltpu.VMEM)
    copies = 21
    f32 = jnp.float32
    synced, sums = pl.pallas_call(
        functools.partial(kernel, blocks, slabs),
        out_shape=(
            jax.ShapeDtypeStruct((FIELDS, tile_count, cells), f32),
            jax.ShapeDtypeStruct((2, EDGE, tile_count), f32),
        ),
        in_specs=[stay] * 5,
        out_specs=(vmem, vmem),
        scratch_shapes=[
            pltpu.VMEM((FIELDS, patches, 8, cells), f32),
            pltpu.VMEM((FIELDS, tile_count, cells), f32),
            pltpu.VMEM((tile_count, cells), jnp.int32),
            pltpu.VMEM((1, patches), jnp.int32),
            pltpu.VMEM((1, patches), jnp.int32),
            pltpu.VMEM((blocks, 8, 128), f32),
            pltpu.VMEM((blocks, FIELDS, 2, patches // 2, cells), f32),
            pltpu.VMEM((tile_count, 512), jnp.bfloat16),
            pltpu.VMEM((EDGE, EDGE, EDGE, tile_count), f32),
            pltpu.VMEM((EDGE, EDGE, EDGE, tile_count), f32),
            pltpu.VMEM((EDGE, EDGE, tile_count), f32),
            pltpu.VMEM((slabs, 2, EDGE, tile_count), f32),
            pltpu.SemaphoreType.DMA((FIELDS + 4,)),
            pltpu.SemaphoreType.DMA((blocks,)),
            pltpu.SemaphoreType.DMA((blocks,)),
            pltpu.SemaphoreType.DMA((copies,)),
            pltpu.SemaphoreType.DMA((copies,)),
            pltpu.SemaphoreType.DMA((slabs,)),
            pltpu.SemaphoreType.DMA((slabs,)),
        ],
        compiler_params=pltpu.CompilerParams(
            collective_id=0, has_side_effects=True, vmem_limit_bytes=VMEM_BYTES
        ),
        name="average_down",
    )(*[
        pltpu.with_memory_space_constraint(x, pltpu.HBM)
        for x in (coarse, fine_fields, owner.reshape(1, patches), target_tile.reshape(1, patches), tags)
    ])
    width = tile_count * EDGE + EDGE
    synced, signature = pl.pallas_call(
        functools.partial(finish, slabs),
        out_shape=(
            jax.ShapeDtypeStruct((FIELDS, tile_count, cells), f32),
            jax.ShapeDtypeStruct((1, width), f32),
        ),
        in_specs=[vmem, vmem],
        out_specs=(stay, stay),
        scratch_shapes=[pltpu.VMEM((1, width), f32), pltpu.SemaphoreType.DMA((1 + FIELDS * PIECES,))],
        compiler_params=pltpu.CompilerParams(vmem_limit_bytes=4 * 1024 * 1024),
        name="write_outputs",
    )(synced, sums)
    return jnp.transpose(synced, (1, 0, 2)), signature


def solution(mesh):
    blocks, slabs = mesh.shape["blk"], mesh.shape["sig"]
    return jax.shard_map(
        functools.partial(shards, blocks, slabs),
        mesh=mesh,
        in_specs=(
            P(("blk", "sig"), None, None),
            P(("blk", "sig"), None, None, None),
            P(("blk", "sig"), None),
            P(("blk", "sig"), None),
            P(("blk", "sig"), None),
        ),
        out_specs=(P(("blk", "sig"), None, None), P("blk", None)),
        check_vma=False,
    )
```
